128 devices in a mesh: seq: 32 (over z, x, core), ch: 4 (over y).
Axes of the slice: x: 4, y: 4, z: 4, core: 2. Of those that a mesh axis runs over, the one named last changes fastest.
Arguments:
- streams: bfloat16 [3, 4096, 4096], P(None, 'seq', 'ch'), may hold values from -6 to 6
- short_taps: float32 [3, 3, 4096], P(None, None, 'ch'), may hold values from -3 to 3
- long_filter: float32 [4096, 4096], P('seq', 'ch'), may hold values from -0.09375 to 0.09375
- skip_gain: float32 [4096], P('ch'), may hold values from -4 to 4
- out_weights: bfloat16 [4096, 8192], P('ch'), may hold values from -0.09375 to 0.09375
Outputs:
- block_out: bfloat16 [4096, 8192], P('seq', 'ch')
The draws below stay inside these ranges and needn't reach their ends.
All inputs are finite; a program needn't handle non-finite values.
Results may differ from the reference program's by a relative error of at most 0.005.
Values may be sent and summed in bfloat16 or wider, within the bound.
No kernel may reach another device: no remote copies, remote signals or barrier semaphores. Data moves between devices by JAX's collectives and lax.ppermute only.
A program may use at most 128 MiB of HBM per device.

```python
import jax
import jax.numpy as jnp

D = 8192
CH = 4096
SHORT = 3
TOKENS = 4096


def block_levels(own_key, extent, shards, smallest, largest):
    def one(position, shards_of):
        draws = jax.random.uniform(jax.random.fold_in(jax.random.fold_in(own_key, 6), position), (shards_of,), jnp.float32, smallest / len(shards), largest / len(shards))
        return jnp.repeat(jnp.exp(draws), extent[position] // shards_of).reshape((-1,) + (1,) * (len(extent) - position - 1))

    gain = one(*shards[0])
    for cut in shards[1:]:
        gain = gain * one(*cut)
    return gain


def noise(stream_key, extent, scale, reach, split=(), kind=jnp.bfloat16):
    array = scale * jax.random.normal(stream_key, extent, jnp.float32)
    if split:
        array = array * block_levels(stream_key, extent, split, -0.22, 0.18)
    return jnp.clip(array, -reach, reach).astype(kind)


def setup_inputs(seed: int = 0) -> dict:
    key_of = jax.random.split(jax.random.key(seed), 6)
    streams = noise(key_of[0], (3, TOKENS, CH), 1.0, 6.0, ((1, 32), (2, 4)))
    short_taps = noise(key_of[1], (3, SHORT, CH), 0.6, 3.0, ((2, 4),), jnp.float32)
    long_filter = noise(key_of[2], (TOKENS, CH), TOKENS ** -0.5, 0.09375, ((0, 32), (1, 4)), jnp.float32)
    skip_gain = noise(key_of[3], (CH,), 1.0, 4.0, ((0, 4),), jnp.float32)
    out_weights = noise(key_of[4], (CH, D), CH ** -0.5, 0.09375, ((0, 4),))
    return {"streams": streams, "short_taps": short_taps, "long_filter": long_filter, "skip_gain": skip_gain, "out_weights": out_weights}


def reference(streams, short_taps, long_filter, skip_gain, out_weights):
    values = streams.astype(jnp.float32)
    padded = jnp.pad(values, ((0, 0), (SHORT - 1, 0), (0, 0)))
    short = jnp.zeros_like(values)
    for offset in range(SHORT):
        window = padded[:, SHORT - 1 - offset:SHORT - 1 - offset + TOKENS, :]
        short = short + short_taps[:, offset][:, None, :] * window
    gated = short[1] * short[2]
    length = 2 * TOKENS
    spectrum = jnp.fft.rfft(gated, n=length, axis=0) * jnp.fft.rfft(long_filter, n=length, axis=0)
    conv = jnp.fft.irfft(spectrum, n=length, axis=0)[:TOKENS].astype(gated.dtype)
    mixed = (short[0] * (conv + skip_gain[None, :] * gated)).astype(jnp.bfloat16)
    return jnp.dot(mixed, out_weights, preferred_element_type=jnp.float32).astype(jnp.bfloat16)
```

```python
import functools
import math

import jax
import jax.numpy as jnp
import numpy as np
from jax import lax
from jax.experimental import pallas as pl
from jax.experimental.pallas import tpu as pltpu
from jax.sharding import PartitionSpec as P

SHORT = 3
STREAMS = 3
ROWS = 128
PARTS = 32
GROUP = 32
SLAB = 16
POINTS = PARTS * ROWS
f32 = jnp.float32
bf16 = jnp.bfloat16


def tables():
    r = np.arange(ROWS)
    angle = 2.0 * np.pi * (np.outer(r, r) % ROWS) / ROWS
    cosine, sine = np.cos(angle), np.sin(angle)
    matrix = np.block([[cosine, -sine], [sine, cosine]])
    high = matrix.astype(np.float32).astype(bf16)
    low = (matrix - high.astype(np.float64)).astype(np.float32).astype(bf16)
    j = np.arange(PARTS)
    twist = 2.0 * np.pi * np.outer(4 * j + 1, r) / (4 * POINTS)
    twists = np.stack([np.cos(twist), np.sin(twist)], axis=1).astype(np.float32)
    return high, low, twists


def turned(value, turns):
    real, imag = value
    eighth = turns * 8 % 8
    if eighth == 0:
        return real, imag
    if eighth == 2:
        return -imag, real
    if eighth == 4:
        return -real, -imag
    if eighth == 6:
        return imag, -real
    if eighth in (1, 3, 5, 7):
        half = math.sqrt(0.5)
        total, apart = (real + imag) * half, (real - imag) * half
        return {1: (apart, total), 3: (-total, apart), 5: (-apart, -total), 7: (total, -apart)}[int(eighth)]
    c, s = math.cos(2.0 * math.pi * turns), math.sin(2.0 * math.pi * turns)
    return real * c - imag * s, real * s + imag * c


def plus(a, b):
    return a[0] + b[0], a[1] + b[1]


def minus(a, b):
    return a[0] - b[0], a[1] - b[1]


def small_transform(values, sign):
    count = len(values)
    if count == 1:
        return values
    even = small_transform(values[0::2], sign)
    odd = small_transform(values[1::2], sign)
    odd = [turned(value, sign * k / count) for k, value in enumerate(odd)]
    return [plus(a, b) for a, b in zip(even, odd)] + [minus(a, b) for a, b in zip(even, odd)]


def exchange_kernel(streams_ref, filter_ref, out_ref):
    groups = out_ref.shape[0]
    for j in range(STREAMS + 1):
        block = streams_ref[j].astype(f32) if j < STREAMS else filter_ref[...]
        turned_block = block.T.astype(bf16).reshape(groups, GROUP, ROWS)
        out_ref[:, j * GROUP : (j + 1) * GROUP, :] = turned_block


def split(value):
    high = value.astype(bf16)
    return high, (value - high.astype(f32)).astype(bf16)


def conv_kernel(x_ref, taps_ref, skip_ref, high_ref, low_ref, twists_ref, out_ref, gated_ref, first_ref, left_ref, back_ref):
    lane = lax.broadcasted_iota(jnp.int32, (SLAB, ROWS), 1)

    def rows_of(j, offset):
        return pl.ds(pl.multiple_of(j * GROUP + offset, SLAB), SLAB)

    def short(stream, offset):
        taps = [taps_ref[stream * SHORT + i, pl.ds(offset, SLAB), :] for i in range(SHORT)]
        before = [jnp.zeros((SLAB, ROWS), f32)] * 2
        for s in range(PARTS):
            now = x_ref[s, rows_of(stream, offset), :].astype(f32)
            moved = [pltpu.roll(now, i, 1) for i in (1, 2)]
            total = taps[0] * now
            for i in (1, 2):
                total = total + taps[i] * jnp.where(lane < i, before[i - 1], moved[i - 1])
            before = moved
            yield total

    def forward(slot, offset, load):
        for a in range(8):
            values = []
            for q in range(4):
                value = load(a + 8 * q)
                angle = -2.0 * math.pi * q / 16
                values.append((value * math.cos(angle), value * math.sin(angle)) if q else (value, jnp.zeros_like(value)))
            for m, value in enumerate(small_transform(values, -1)):
                real, imag = turned(value, -a * (4 * m + 1) / 128)
                first_ref[m, a, 0] = real
                first_ref[m, a, 1] = imag
        for m in range(4):
            values = [(first_ref[m, a, 0], first_ref[m, a, 1]) for a in range(8)]
            for p, (real, imag) in enumerate(small_transform(values, -1)):
                j = 4 * p + m
                c, s = twists_ref[j, 0][None, :], twists_ref[j, 1][None, :]
                for half, part in enumerate((real * c + imag * s, imag * c - real * s)):
                    high, low = split(part)
                    left_ref[slot, 0, rows_of(j, offset), half * ROWS : (half + 1) * ROWS] = high
                    left_ref[slot, 1, rows_of(j, offset), half * ROWS : (half + 1) * ROWS] = low

    @pl.loop(0, GROUP // SLAB)
    def _(step):
        offset = pl.multiple_of(step * SLAB, SLAB)
        for s, (key, value) in enumerate(zip(short(1, offset), short(2, offset))):
            gated_ref[s, pl.ds(offset, SLAB), :] = key * value
        forward(0, offset, lambda s: gated_ref[s, pl.ds(offset, SLAB), :])
        forward(1, offset, lambda s: x_ref[s, rows_of(STREAMS, offset), :].astype(f32))

    def product(high, low):
        total = jnp.dot(low, high_ref[...], preferred_element_type=f32)
        total = total + jnp.dot(high, low_ref[...], preferred_element_type=f32)
        return total + jnp.dot(high, high_ref[...], preferred_element_type=f32)

    block = 256

    @pl.loop(0, PARTS * GROUP // block)
    def _(step):
        rows = pl.ds(pl.multiple_of(step * block, block), block)
        signal = product(left_ref[0, 0, rows, :], left_ref[0, 1, rows, :])
        taps = product(left_ref[1, 0, rows, :], left_ref[1, 1, rows, :])
        a, b = signal[:, :ROWS], signal[:, ROWS:]
        c, d = taps[:, :ROWS], taps[:, ROWS:]
        real, imag = split((a * c - b * d) * (1.0 / POINTS)), split((a * d + b * c) * (-1.0 / POINTS))
        high = jnp.concatenate([real[0], imag[0]], axis=1)
        low = jnp.concatenate([real[1], imag[1]], axis=1)
        back_ref[rows, :] = product(high, low)

    @pl.loop(0, GROUP // SLAB)
    def _(step):
        offset = pl.multiple_of(step * SLAB, SLAB)
        for m in range(4):
            values = []
            for p in range(8):
                j = 4 * p + m
                real = back_ref[rows_of(j, offset), :ROWS]
                imag = -back_ref[rows_of(j, offset), ROWS:]
                c, s = twists_ref[j, 0][None, :], twists_ref[j, 1][None, :]
                values.append((real * c - imag * s, real * s + imag * c))
            for a, value in enumerate(small_transform(values, 1)):
                real, imag = turned(value, a * (4 * m + 1) / 128)
                first_ref[m, a, 0] = real
                first_ref[m, a, 1] = imag
        skip = skip_ref[pl.ds(offset, SLAB), :]
        for a in range(8):
            values = [(first_ref[m, a, 0], first_ref[m, a, 1]) for m in range(4)]
            for q, (real, imag) in enumerate(small_transform(values, 1)):
                angle = 2.0 * math.pi * q / 16
                conv = real * math.cos(angle) - imag * math.sin(angle) if q else real
                s = a + 8 * q
                gated = gated_ref[s, pl.ds(offset, SLAB), :]
                gated_ref[s, pl.ds(offset, SLAB), :] = conv + skip * gated
        for s, query in enumerate(short(0, offset)):
            out_ref[s, pl.ds(offset, SLAB), :] = (query * gated_ref[s, pl.ds(offset, SLAB), :]).astype(bf16)


def far_kernel(index_ref, mixed_ref, weights_ref, out_ref, rows_ref):
    @pl.when(pl.program_id(0) == 0)
    def _():
        rows_ref[...] = mixed_ref[...].astype(f32).T.astype(bf16)

    out_ref[0] = jnp.dot(rows_ref[...], weights_ref[...], preferred_element_type=f32).astype(out_ref.dtype)


def near_kernel(index_ref, rows_ref, weights_ref, out_ref):
    out_ref[0] = jnp.dot(rows_ref[...], weights_ref[...], preferred_element_type=f32).astype(out_ref.dtype)


def adding_kernel(index_ref, rows_ref, weights_ref, up_ref, down_ref, out_ref):
    half = pl.num_programs(0) // 2
    arrived = jnp.where(pl.program_id(0) < half, up_ref[...], down_ref[...]).astype(f32)
    total = jnp.dot(rows_ref[...], weights_ref[...], preferred_element_type=f32)
    out_ref[0] = (total + arrived).astype(out_ref.dtype)


WIDE = 512


def share(kernel, index, rows, weights, dtype, arrived=(), first=False):
    count = index.shape[0]
    depth = weights.shape[0]
    half = count // 2
    row_spec = pl.BlockSpec(rows.shape, lambda i, index: (0, 0))
    in_specs = [row_spec, pl.BlockSpec((depth, WIDE), lambda i, index: (0, index[i]))]
    if arrived:
        in_specs.append(pl.BlockSpec((ROWS, WIDE), lambda i, index: (0, jnp.minimum(i, half - 1))))
        in_specs.append(pl.BlockSpec((ROWS, WIDE), lambda i, index: (0, jnp.maximum(i - half, 0))))
    out_shape = [jax.ShapeDtypeStruct((2, ROWS, half * WIDE), dtype)]
    out_specs = [pl.BlockSpec((1, ROWS, WIDE), lambda i, index: (i // half, 0, i % half))]
    if first:
        out_shape.append(jax.ShapeDtypeStruct((ROWS, depth), bf16))
        out_specs.append(pl.BlockSpec((ROWS, depth), lambda i, index: (0, 0)))
    return pl.pallas_call(
        kernel,
        grid_spec=pltpu.PrefetchScalarGridSpec(
            num_scalar_prefetch=1, grid=(count,), in_specs=in_specs, out_specs=out_specs
        ),
        out_shape=out_shape,
        cost_estimate=pl.CostEstimate(
            flops=2 * ROWS * depth * count * WIDE, bytes_accessed=2 * depth * count * WIDE, transcendentals=0
        ),
        compiler_params=pltpu.CompilerParams(vmem_limit_bytes=32 * 2**20),
    )(index, rows, weights, *arrived)


def project(mixed, weights):
    ring = lax.axis_size("ch")
    me = lax.axis_index("ch")
    up = [(i, (i + 1) % ring) for i in range(ring)]
    down = [(i, (i - 1) % ring) for i in range(ring)]
    blocks = weights.shape[1] // ring // WIDE
    half = blocks // 2

    def numbers(away, start, stop):
        return (me + away) % ring * blocks + jnp.arange(start, stop, dtype=jnp.int32)

    far, rows = share(far_kernel, numbers(2, 0, blocks), mixed, weights, bf16, first=True)
    far_up = lax.ppermute(far[0], "ch", up)
    far_down = lax.ppermute(far[1], "ch", down)
    index = jnp.concatenate([numbers(1, half, blocks), numbers(-1, 0, half)])
    (near,) = share(near_kernel, index, rows, weights, bf16)
    near_up = lax.ppermute(near[0], "ch", up)
    near_down = lax.ppermute(near[1], "ch", down)
    index = jnp.concatenate([numbers(1, 0, half), numbers(-1, half, blocks)])
    (both,) = share(adding_kernel, index, rows, weights, bf16, arrived=(far_up, far_down))
    both_up = lax.ppermute(both[0], "ch", up)
    both_down = lax.ppermute(both[1], "ch", down)
    (own,) = share(near_kernel, numbers(0, 0, blocks), rows, weights, f32)
    left = own[0] + both_up.astype(f32) + near_down.astype(f32)
    right = own[1] + near_up.astype(f32) + both_down.astype(f32)
    return jnp.concatenate([left, right], axis=1).astype(bf16)


def on_device(streams, short_taps, long_filter, skip_gain, out_weights):
    channels = streams.shape[2]
    wide = 256
    packed = pl.pallas_call(
        exchange_kernel,
        grid=(channels // wide,),
        in_specs=[
            pl.BlockSpec((STREAMS, ROWS, wide), lambda i: (0, 0, i)),
            pl.BlockSpec((ROWS, wide), lambda i: (0, i)),
        ],
        out_specs=pl.BlockSpec((wide // GROUP, (STREAMS + 1) * GROUP, ROWS), lambda i: (i, 0, 0)),
        out_shape=jax.ShapeDtypeStruct((PARTS, (STREAMS + 1) * GROUP, ROWS), bf16),
    )(streams, long_filter)
    first = lax.axis_index("seq") * GROUP
    taps = lax.dynamic_slice_in_dim(short_taps.reshape(STREAMS * SHORT, channels), first, GROUP, 1)
    taps = jnp.broadcast_to(taps[:, :, None], (STREAMS * SHORT, GROUP, ROWS))
    skip = jnp.broadcast_to(lax.dynamic_slice_in_dim(skip_gain, first, GROUP, 0)[:, None], (GROUP, ROWS))
    arrived = lax.all_to_all(packed, "seq", 0, 0, tiled=True)
    high, low, twists = tables()
    whole = pl.BlockSpec(memory_space=pltpu.VMEM)
    mixed = pl.pallas_call(
        conv_kernel,
        in_specs=[whole] * 6,
        out_specs=whole,
        out_shape=jax.ShapeDtypeStruct((PARTS, GROUP, ROWS), bf16),
        scratch_shapes=[
            pltpu.VMEM((PARTS, GROUP, ROWS), f32),
            pltpu.VMEM((4, 8, 2, SLAB, ROWS), f32),
            pltpu.VMEM((2, 2, PARTS * GROUP, 2 * ROWS), bf16),
            pltpu.VMEM((PARTS * GROUP, 2 * ROWS), f32),
        ],
        compiler_params=pltpu.CompilerParams(vmem_limit_bytes=32 * 2**20),
    )(arrived, taps, skip, jnp.asarray(high), jnp.asarray(low), jnp.asarray(twists))
    mixed = lax.all_to_all(mixed, "seq", 0, 0, tiled=True)
    return project(mixed.reshape(channels, ROWS), out_weights)


def solution(mesh):
    return jax.shard_map(
        on_device,
        mesh=mesh,
        in_specs=(
            P(None, "seq", "ch"),
            P(None, None, "ch"),
            P("seq", "ch"),
            P("ch"),
            P("ch", None),
        ),
        out_specs=P("seq", "ch"),
        check_vma=False,
    )
```

```python
import math

import jax
import jax.numpy as jnp
import numpy as np
from jax import lax
from jax.experimental import pallas as pl
from jax.experimental.pallas import tpu as pltpu
from jax.sharding import PartitionSpec as P

SHORT = 3
ROWS = 128
PARTS = 32
GROUP = 32
SLAB = 16
POINTS = PARTS * ROWS
f32 = jnp.float32
bf16 = jnp.bfloat16


def tables():
    r = np.arange(ROWS)
    angle = 2.0 * np.pi * (np.outer(r, r) % ROWS) / ROWS
    cosine, sine = np.cos(angle), np.sin(angle)
    matrix = np.block([[cosine, -sine], [sine, cosine]])
    high = matrix.astype(np.float32).astype(bf16)
    low = (matrix - high.astype(np.float64)).astype(np.float32).astype(bf16)
    j = np.arange(PARTS)
    twist = 2.0 * np.pi * np.outer(4 * j + 1, r) / (4 * POINTS)
    twists = np.stack([np.cos(twist), np.sin(twist)], axis=1).astype(np.float32)
    return high, low, twists


def turned(value, turns):
    real, imag = value
    eighth = turns * 8 % 8
    if eighth == 0:
        return real, imag
    if eighth == 2:
        return -imag, real
    if eighth == 4:
        return -real, -imag
    if eighth == 6:
        return imag, -real
    if eighth in (1, 3, 5, 7):
        half = math.sqrt(0.5)
        total, apart = (real + imag) * half, (real - imag) * half
        return {1: (apart, total), 3: (-total, apart), 5: (-apart, -total), 7: (total, -apart)}[int(eighth)]
    c, s = math.cos(2.0 * math.pi * turns), math.sin(2.0 * math.pi * turns)
    return real * c - imag * s, real * s + imag * c


def plus(a, b):
    return a[0] + b[0], a[1] + b[1]


def minus(a, b):
    return a[0] - b[0], a[1] - b[1]


def small_transform(values, sign):
    count = len(values)
    if count == 1:
        return values
    even = small_transform(values[0::2], sign)
    odd = small_transform(values[1::2], sign)
    odd = [turned(value, sign * k / count) for k, value in enumerate(odd)]
    return [plus(a, b) for a, b in zip(even, odd)] + [minus(a, b) for a, b in zip(even, odd)]


def exchange_kernel(streams_ref, filter_ref, out_ref, token_ref, rows_ref, taps_ref, sems):
    copies = [pltpu.make_async_copy(streams_ref.at[i + 1], rows_ref.at[i], sems.at[i]) for i in range(SENT - 1)]
    copies.append(pltpu.make_async_copy(filter_ref, taps_ref, sems.at[SENT - 1]))
    for copy in copies:
        copy.start()
    token_ref[...] = jnp.zeros_like(token_ref)
    wide = 8 * GROUP
    for j, copy in enumerate(copies):
        copy.wait()
        for first in range(0, PARTS * GROUP, wide):
            here = slice(first, first + wide)
            block = rows_ref[j, :, here] if j < SENT - 1 else taps_ref[:, here].astype(bf16)
            parts = pl.ds(first // GROUP, wide // GROUP)
            out_ref[parts, j * GROUP : (j + 1) * GROUP, :] = block.T.reshape(wide // GROUP, GROUP, ROWS)


def stage_kernel(*refs):
    sems = refs[-1]
    count = sems.shape[0]
    copies = [
        pltpu.make_async_copy(source, target, sems.at[i])
        for i, (source, target) in enumerate(zip(refs[1 : 1 + count], refs[1 + count : -1]))
    ]
    for copy in copies:
        copy.start()
    for copy in copies:
        copy.wait()


def query_kernel(query_ref, earlier_ref, taps_ref, out_ref):
    now = query_ref[0].astype(f32)
    row = lax.broadcasted_iota(jnp.int32, now.shape, 0)
    last, before_last = earlier_ref[1:2, :], earlier_ref[0:1, :]
    one = jnp.where(row == 0, last, pltpu.roll(now, 1, 0))
    two = jnp.where(row == 0, before_last, jnp.where(row == 1, last, pltpu.roll(now, 2, 0)))
    out_ref[...] = taps_ref[0, 0:1, :] * now + taps_ref[0, 1:2, :] * one + taps_ref[0, 2:3, :] * two


def split(value):
    high = value.astype(bf16)
    return high, (value - high.astype(f32)).astype(bf16)


def conv_kernel(x_ref, taps_ref, skip_ref, high_ref, low_ref, twists_ref, out_ref, gated_ref, first_ref, left_ref, back_ref):
    lane = lax.broadcasted_iota(jnp.int32, (SLAB, ROWS), 1)

    def rows_of(j, offset):
        return pl.ds(pl.multiple_of(j * GROUP + offset, SLAB), SLAB)

    def short(stream, offset):
        taps = [taps_ref[stream * SHORT + i, pl.ds(offset, SLAB), :] for i in range(SHORT)]
        before = [jnp.zeros((SLAB, ROWS), f32)] * 2
        for s in range(PARTS):
            now = x_ref[s, rows_of(stream, offset), :].astype(f32)
            moved = [pltpu.roll(now, i, 1) for i in (1, 2)]
            total = taps[0] * now
            for i in (1, 2):
                total = total + taps[i] * jnp.where(lane < i, before[i - 1], moved[i - 1])
            before = moved
            yield total

    def forward(slot, offset, load):
        for a in range(8):
            values = []
            for q in range(4):
                value = load(a + 8 * q)
                angle = -2.0 * math.pi * q / 16
                values.append((value * math.cos(angle), value * math.sin(angle)) if q else (value, jnp.zeros_like(value)))
            for m, value in enumerate(small_transform(values, -1)):
                real, imag = turned(value, -a * (4 * m + 1) / 128)
                first_ref[m, a, 0] = real
                first_ref[m, a, 1] = imag
        for m in range(4):
            values = [(first_ref[m, a, 0], first_ref[m, a, 1]) for a in range(8)]
            for p, (real, imag) in enumerate(small_transform(values, -1)):
                j = 4 * p + m
                c, s = twists_ref[j, 0][None, :], twists_ref[j, 1][None, :]
                for half, part in enumerate((real * c + imag * s, imag * c - real * s)):
                    high, low = split(part)
                    left_ref[slot, 0, rows_of(j, offset), half * ROWS : (half + 1) * ROWS] = high
                    left_ref[slot, 1, rows_of(j, offset), half * ROWS : (half + 1) * ROWS] = low

    @pl.loop(0, GROUP // SLAB)
    def _(step):
        offset = pl.multiple_of(step * SLAB, SLAB)
        for s, (key, value) in enumerate(zip(short(0, offset), short(1, offset))):
            gated_ref[s, pl.ds(offset, SLAB), :] = key * value
        forward(0, offset, lambda s: gated_ref[s, pl.ds(offset, SLAB), :])
        forward(1, offset, lambda s: x_ref[s, rows_of(SENT - 1, offset), :].astype(f32))

    def product(high, low):
        total = jnp.dot(low, high_ref[...], preferred_element_type=f32)
        total = total + jnp.dot(high, low_ref[...], preferred_element_type=f32)
        return total + jnp.dot(high, high_ref[...], preferred_element_type=f32)

    block = 256

    @pl.loop(0, PARTS * GROUP // block)
    def _(step):
        rows = pl.ds(pl.multiple_of(step * block, block), block)
        signal = product(left_ref[0, 0, rows, :], left_ref[0, 1, rows, :])
        taps = product(left_ref[1, 0, rows, :], left_ref[1, 1, rows, :])
        a, b = signal[:, :ROWS], signal[:, ROWS:]
        c, d = taps[:, :ROWS], taps[:, ROWS:]
        real, imag = split((a * c - b * d) * (1.0 / POINTS)), split((a * d + b * c) * (-1.0 / POINTS))
        high = jnp.concatenate([real[0], imag[0]], axis=1)
        low = jnp.concatenate([real[1], imag[1]], axis=1)
        back_ref[rows, :] = product(high, low)

    @pl.loop(0, GROUP // SLAB)
    def _(step):
        offset = pl.multiple_of(step * SLAB, SLAB)
        for m in range(4):
            values = []
            for p in range(8):
                j = 4 * p + m
                real = back_ref[rows_of(j, offset), :ROWS]
                imag = -back_ref[rows_of(j, offset), ROWS:]
                c, s = twists_ref[j, 0][None, :], twists_ref[j, 1][None, :]
                values.append((real * c - imag * s, real * s + imag * c))
            for a, value in enumerate(small_transform(values, 1)):
                real, imag = turned(value, a * (4 * m + 1) / 128)
                first_ref[m, a, 0] = real
                first_ref[m, a, 1] = imag
        skip = skip_ref[pl.ds(offset, SLAB), :]
        for a in range(8):
            values = [(first_ref[m, a, 0], first_ref[m, a, 1]) for m in range(4)]
            for q, (real, imag) in enumerate(small_transform(values, 1)):
                angle = 2.0 * math.pi * q / 16
                conv = real * math.cos(angle) - imag * math.sin(angle) if q else real
                s = a + 8 * q
                gated = gated_ref[s, pl.ds(offset, SLAB), :]
                out_ref[s, pl.ds(offset, SLAB), :] = (conv + skip * gated).astype(bf16)


def fetch(weights_ref, target_ref, sems, blocks):
    copies = []
    for i, block in enumerate(blocks):
        source = weights_ref.at[:, pl.ds(pl.multiple_of(block * WIDE, WIDE), WIDE)]
        copies.append(pltpu.make_async_copy(source, target_ref.at[:, i * WIDE : (i + 1) * WIDE], sems.at[i]))
    for copy in copies:
        copy.start()
    return copies


def part_of(rows_ref, held_ref, i):
    return jnp.dot(rows_ref[...], held_ref[:, i * WIDE : (i + 1) * WIDE], preferred_element_type=f32)


def first_block(me_ref, away):
    return (me_ref[0] + away) % RING * BLOCKS


def far_kernel(me_ref, outer_ref, query_ref, weights_ref, up_ref, down_ref, rows_ref, held_ref, sems):
    away = first_block(me_ref, 2)
    copies = fetch(weights_ref, held_ref, sems, [away + i for i in range(BLOCKS)])
    rows_ref[...] = (query_ref[...] * outer_ref[...].astype(f32).T).astype(bf16)
    for i, copy in enumerate(copies):
        copy.wait()
        out_ref = up_ref if i < HALF else down_ref
        out_ref[:, i % HALF * WIDE : (i % HALF + 1) * WIDE] = part_of(rows_ref, held_ref, i).astype(bf16)


def near_kernel(me_ref, rows_ref, weights_ref, up_ref, down_ref, later_ref, held_ref, sems):
    above, below = first_block(me_ref, 1), first_block(me_ref, RING - 1)
    now = [above + HALF + i for i in range(HALF)] + [below + i for i in range(HALF)]
    later = [above + i for i in range(HALF)] + [below + HALF + i for i in range(HALF)]
    copies = fetch(weights_ref, held_ref, sems, now)
    more = fetch(weights_ref, later_ref, sems.at[BLOCKS:], later)
    for i, copy in enumerate(copies):
        copy.wait()
        out_ref = up_ref if i < HALF else down_ref
        out_ref[:, i % HALF * WIDE : (i % HALF + 1) * WIDE] = part_of(rows_ref, held_ref, i).astype(bf16)
    for copy in more:
        copy.wait()


def adding_kernel(rows_ref, held_ref, far_up_ref, far_down_ref, up_ref, down_ref):
    for i in range(BLOCKS):
        out_ref, arrived_ref = (up_ref, far_up_ref) if i < HALF else (down_ref, far_down_ref)
        here = slice(i % HALF * WIDE, (i % HALF + 1) * WIDE)
        out_ref[:, here] = (part_of(rows_ref, held_ref, i) + arrived_ref[:, here].astype(f32)).astype(bf16)


def own_kernel(me_ref, rows_ref, near_up_ref, near_down_ref, weights_ref, out_ref, held_ref, sems):
    mine = first_block(me_ref, 0)
    copies = fetch(weights_ref, held_ref, sems, [mine + i for i in range(BLOCKS)])
    for i, copy in enumerate(copies):
        copy.wait()
        arrived_ref = near_down_ref if i < HALF else near_up_ref
        here = slice(i % HALF * WIDE, (i % HALF + 1) * WIDE)
        out_ref[:, i * WIDE : (i + 1) * WIDE] = part_of(rows_ref, held_ref, i) + arrived_ref[:, here].astype(f32)


def last_kernel(own_ref, both_up_ref, both_down_ref, out_ref):
    middle = out_ref.shape[1] // 2
    for here, arrived_ref in ((slice(0, middle), both_up_ref), (slice(middle, 2 * middle), both_down_ref)):
        out_ref[:, here] = (own_ref[:, here] + arrived_ref[...].astype(f32)).astype(bf16)


RING = 4
WIDE = 512
BLOCKS = 4
HALF = BLOCKS // 2
SENT = 3
VMEM = pl.BlockSpec(memory_space=pltpu.VMEM)
SMEM = pl.BlockSpec(memory_space=pltpu.SMEM)
HBM = pl.BlockSpec(memory_space=pltpu.HBM)


def share(kernel, arrays, outs, fetched=0):
    depth = arrays[-1].shape[0]
    arrays, specs = list(arrays), [SMEM if array.ndim == 1 else VMEM for array in arrays]
    scratch = []
    if fetched:
        arrays[-1] = pltpu.with_memory_space_constraint(arrays[-1], pltpu.HBM)
        specs[-1] = HBM
        scratch = [pltpu.VMEM((depth, BLOCKS * WIDE), bf16), pltpu.SemaphoreType.DMA((fetched,))]
    return pl.pallas_call(
        kernel,
        in_specs=specs,
        out_specs=[VMEM] * len(outs),
        out_shape=[pltpu.VMEM(shape, dtype) for shape, dtype in outs],
        scratch_shapes=scratch,
        cost_estimate=pl.CostEstimate(flops=2**32, bytes_accessed=2**22, transcendentals=0),
        compiler_params=pltpu.CompilerParams(vmem_limit_bytes=16 * 2**20),
    )(*arrays)


def project(outer, query, weights):
    me = lax.axis_index("ch").astype(jnp.int32).reshape(1)
    up = [(i, (i + 1) % RING) for i in range(RING)]
    down = [(i, (i - 1) % RING) for i in range(RING)]
    half = ((ROWS, HALF * WIDE), bf16)
    held = ((weights.shape[0], BLOCKS * WIDE), bf16)
    far_up, far_down, rows = share(
        far_kernel, (me, outer, query, weights), [half, half, (query.shape, bf16)], BLOCKS
    )
    far_up = lax.ppermute(far_up, "ch", up)
    far_down = lax.ppermute(far_down, "ch", down)
    near_up, near_down, later = share(near_kernel, (me, rows, weights), [half, half, held], 2 * BLOCKS)
    near_up = lax.ppermute(near_up, "ch", up)
    near_down = lax.ppermute(near_down, "ch", down)
    both_up, both_down = share(adding_kernel, (rows, later, far_up, far_down), [half, half])
    both_up = lax.ppermute(both_up, "ch", up)
    both_down = lax.ppermute(both_down, "ch", down)
    (own,) = share(
        own_kernel, (me, rows, near_up, near_down, weights), [((ROWS, BLOCKS * WIDE), f32)], BLOCKS
    )
    return pl.pallas_call(
        last_kernel,
        in_specs=[VMEM] * 3,
        out_specs=VMEM,
        out_shape=jax.ShapeDtypeStruct((ROWS, BLOCKS * WIDE), bf16),
        compiler_params=pltpu.CompilerParams(vmem_limit_bytes=16 * 2**20),
    )(own, both_up, both_down)


def stage(after, *arrays):
    arrays = [pltpu.with_memory_space_constraint(array, pltpu.HBM) for array in arrays]
    return pl.pallas_call(
        stage_kernel,
        in_specs=[pl.BlockSpec(memory_space=pl.ANY)] + [HBM] * len(arrays),
        out_specs=[VMEM] * len(arrays),
        out_shape=[pltpu.VMEM(array.shape, array.dtype) for array in arrays],
        scratch_shapes=[pltpu.SemaphoreType.DMA((len(arrays),))],
        compiler_params=pltpu.CompilerParams(vmem_limit_bytes=16 * 2**20),
    )(after, *arrays)


def on_device(streams, short_taps, long_filter, skip_gain, out_weights):
    channels = streams.shape[2]
    packed, token = pl.pallas_call(
        exchange_kernel,
        in_specs=[HBM, HBM],
        out_specs=[VMEM, VMEM],
        out_shape=[
            jax.ShapeDtypeStruct((PARTS, SENT * GROUP, ROWS), bf16),
            jax.ShapeDtypeStruct((8, ROWS), f32),
        ],
        scratch_shapes=[
            pltpu.VMEM((SENT - 1, ROWS, channels), bf16),
            pltpu.VMEM((ROWS, channels), f32),
            pltpu.SemaphoreType.DMA((SENT,)),
        ],
        compiler_params=pltpu.CompilerParams(vmem_limit_bytes=8 * 2**20),
    )(*(pltpu.with_memory_space_constraint(array, pltpu.HBM) for array in (streams, long_filter)))
    high, low, twists = (jnp.asarray(table) for table in tables())
    high, low, twists = stage(token, high, low, twists)
    arrived = lax.all_to_all(packed, "seq", 0, 0, tiled=True)
    earlier = lax.ppermute(streams[0, ROWS - (SHORT - 1) :], "seq", [(i, i + 1) for i in range(PARTS - 1)])
    query = pl.pallas_call(
        query_kernel,
        grid=(1,),
        in_specs=[
            pl.BlockSpec((1, ROWS, channels), lambda i: (0, 0, 0)),
            pl.BlockSpec((SHORT - 1, channels), lambda i: (0, 0)),
            pl.BlockSpec(short_taps.shape, lambda i: (0, 0, 0)),
        ],
        out_specs=pl.BlockSpec((ROWS, channels), lambda i: (0, 0)),
        out_shape=pltpu.VMEM((ROWS, channels), f32),
        compiler_params=pltpu.CompilerParams(vmem_limit_bytes=8 * 2**20),
    )(streams, earlier.astype(f32), short_taps)
    first = lax.axis_index("seq") * GROUP
    taps = lax.dynamic_slice_in_dim(short_taps[1:].reshape((SENT - 1) * SHORT, channels), first, GROUP, 1)
    taps = jnp.broadcast_to(taps[:, :, None], ((SENT - 1) * SHORT, GROUP, ROWS))
    skip = jnp.broadcast_to(lax.dynamic_slice_in_dim(skip_gain, first, GROUP, 0)[:, None], (GROUP, ROWS))
    outer = pl.pallas_call(
        conv_kernel,
        in_specs=[VMEM] * 6,
        out_specs=VMEM,
        out_shape=jax.ShapeDtypeStruct((PARTS, GROUP, ROWS), bf16),
        scratch_shapes=[
            pltpu.VMEM((PARTS, GROUP, ROWS), f32),
            pltpu.VMEM((4, 8, 2, SLAB, ROWS), f32),
            pltpu.VMEM((2, 2, PARTS * GROUP, 2 * ROWS), bf16),
            pltpu.VMEM((PARTS * GROUP, 2 * ROWS), f32),
        ],
        compiler_params=pltpu.CompilerParams(vmem_limit_bytes=16 * 2**20),
    )(arrived, taps, skip, high, low, twists)
    outer = lax.all_to_all(outer, "seq", 0, 0, tiled=True)
    return project(outer.reshape(channels, ROWS), query, out_weights)


def solution(mesh):
    return jax.shard_map(
        on_device,
        mesh=mesh,
        in_specs=(
            P(None, "seq", "ch"),
            P(None, None, "ch"),
            P("seq", "ch"),
            P("ch"),
            P("ch", None),
        ),
        out_specs=P("seq", "ch"),
        check_vma=False,
    )
```

```python
import functools
import math

import jax
import jax.numpy as jnp
import numpy as np
from jax import lax
from jax.experimental import pallas as pl
from jax.experimental.pallas import tpu as pltpu
from jax.sharding import PartitionSpec as P

SHORT = 3
ROWS = 128
PARTS = 32
GROUP = 32
SLAB = 16
POINTS = PARTS * ROWS
f32 = jnp.float32
bf16 = jnp.bfloat16


def tables():
    r = np.arange(ROWS)
    angle = 2.0 * np.pi * (np.outer(r, r) % ROWS) / ROWS
    cosine, sine = np.cos(angle), np.sin(angle)
    matrix = np.block([[cosine, -sine], [sine, cosine]])
    high = matrix.astype(np.float32).astype(bf16)
    low = (matrix - high.astype(np.float64)).astype(np.float32).astype(bf16)
    j = np.arange(PARTS)
    twist = 2.0 * np.pi * np.outer(4 * j + 1, r) / (4 * POINTS)
    twists = np.stack([np.cos(twist), np.sin(twist)], axis=1).astype(np.float32)
    return high, low, twists


def turned(value, turns):
    real, imag = value
    eighth = turns * 8 % 8
    if eighth == 0:
        return real, imag
    if eighth == 2:
        return -imag, real
    if eighth == 4:
        return -real, -imag
    if eighth == 6:
        return imag, -real
    if eighth in (1, 3, 5, 7):
        half = math.sqrt(0.5)
        total, apart = (real + imag) * half, (real - imag) * half
        return {1: (apart, total), 3: (-total, apart), 5: (-apart, -total), 7: (total, -apart)}[int(eighth)]
    c, s = math.cos(2.0 * math.pi * turns), math.sin(2.0 * math.pi * turns)
    return real * c - imag * s, real * s + imag * c


def plus(a, b):
    return a[0] + b[0], a[1] + b[1]


def minus(a, b):
    return a[0] - b[0], a[1] - b[1]


def small_transform(values, sign):
    count = len(values)
    if count == 1:
        return values
    even = small_transform(values[0::2], sign)
    odd = small_transform(values[1::2], sign)
    odd = [turned(value, sign * k / count) for k, value in enumerate(odd)]
    return [plus(a, b) for a, b in zip(even, odd)] + [minus(a, b) for a, b in zip(even, odd)]


def exchange_kernel(streams_ref, filter_ref, out_ref, edge_ref, rows_ref, taps_ref, sems):
    copies = [pltpu.make_async_copy(streams_ref.at[i + 1], rows_ref.at[i], sems.at[i]) for i in range(SENT - 1)]
    copies.append(pltpu.make_async_copy(filter_ref, taps_ref, sems.at[SENT - 1]))
    edge = pltpu.make_async_copy(streams_ref.at[0, ROWS - EDGE :], edge_ref, sems.at[SENT])
    for copy in copies:
        copy.start()
    edge.start()
    wide = 8 * GROUP
    for j, copy in enumerate(copies):
        copy.wait()
        for first in range(0, PARTS * GROUP, wide):
            here = slice(first, first + wide)
            block = rows_ref[j, :, here] if j < SENT - 1 else taps_ref[:, here].astype(bf16)
            parts = pl.ds(first // GROUP, wide // GROUP)
            out_ref[parts, j * GROUP : (j + 1) * GROUP, :] = block.T.reshape(wide // GROUP, GROUP, ROWS)
    edge.wait()


def stage_kernel(*refs):
    sems = refs[-1]
    count = sems.shape[0]
    copies = [
        pltpu.make_async_copy(source, target, sems.at[i])
        for i, (source, target) in enumerate(zip(refs[1 : 1 + count], refs[1 + count : -1]))
    ]
    for copy in copies:
        copy.start()
    for copy in copies:
        copy.wait()


def query_kernel(streams_ref, edge_ref, taps_ref, held_ref, out_ref, rows_ref, sem):
    copy = pltpu.make_async_copy(streams_ref.at[0], rows_ref, sem.at[0])
    copy.start()
    copy.wait()
    now = rows_ref[...].astype(f32)
    earlier = edge_ref[...].astype(f32)
    row = lax.broadcasted_iota(jnp.int32, now.shape, 0)
    last, before_last = earlier[EDGE - 1 :, :], earlier[EDGE - 2 : EDGE - 1, :]
    one = jnp.where(row == 0, last, pltpu.roll(now, 1, 0))
    two = jnp.where(row == 0, before_last, jnp.where(row == 1, last, pltpu.roll(now, 2, 0)))
    out_ref[...] = taps_ref[0, 0:1, :] * now + taps_ref[0, 1:2, :] * one + taps_ref[0, 2:3, :] * two


def split(value):
    high = value.astype(bf16)
    return high, (value - high.astype(f32)).astype(bf16)


def conv_kernel(
    me_ref, x_ref, taps_ref, skip_ref, high_ref, low_ref, twists_ref, weights_ref,
    out_ref, held_ref, gated_ref, first_ref, left_ref, back_ref, sems,
):
    copies = fetch(weights_ref, held_ref, sems, 2, me_ref, LEFT)
    lane = lax.broadcasted_iota(jnp.int32, (SLAB, ROWS), 1)

    def rows_of(j, offset):
        return pl.ds(pl.multiple_of(j * GROUP + offset, SLAB), SLAB)

    def short(stream, offset):
        taps = [taps_ref[stream * SHORT + i, pl.ds(offset, SLAB), :] for i in range(SHORT)]
        before = [jnp.zeros((SLAB, ROWS), f32)] * 2
        for s in range(PARTS):
            now = x_ref[s, rows_of(stream, offset), :].astype(f32)
            moved = [pltpu.roll(now, i, 1) for i in (1, 2)]
            total = taps[0] * now
            for i in (1, 2):
                total = total + taps[i] * jnp.where(lane < i, before[i - 1], moved[i - 1])
            before = moved
            yield total

    def forward(slot, offset, load):
        for a in range(8):
            values = []
            for q in range(4):
                value = load(a + 8 * q)
                angle = -2.0 * math.pi * q / 16
                values.append((value * math.cos(angle), value * math.sin(angle)) if q else (value, jnp.zeros_like(value)))
            for m, value in enumerate(small_transform(values, -1)):
                real, imag = turned(value, -a * (4 * m + 1) / 128)
                first_ref[m, a, 0] = real
                first_ref[m, a, 1] = imag
        for m in range(4):
            values = [(first_ref[m, a, 0], first_ref[m, a, 1]) for a in range(8)]
            for p, (real, imag) in enumerate(small_transform(values, -1)):
                j = 4 * p + m
                c, s = twists_ref[j, 0][None, :], twists_ref[j, 1][None, :]
                for half, part in enumerate((real * c + imag * s, imag * c - real * s)):
                    high, low = split(part)
                    left_ref[slot, 0, rows_of(j, offset), half * ROWS : (half + 1) * ROWS] = high
                    left_ref[slot, 1, rows_of(j, offset), half * ROWS : (half + 1) * ROWS] = low

    @pl.loop(0, GROUP // SLAB)
    def _(step):
        offset = pl.multiple_of(step * SLAB, SLAB)
        for s, (key, value) in enumerate(zip(short(0, offset), short(1, offset))):
            gated_ref[s, pl.ds(offset, SLAB), :] = key * value
        forward(0, offset, lambda s: gated_ref[s, pl.ds(offset, SLAB), :])
        forward(1, offset, lambda s: x_ref[s, rows_of(SENT - 1, offset), :].astype(f32))

    matrix = jnp.concatenate([high_ref[...], low_ref[...], high_ref[...]], axis=0)

    def product(high, low):
        return jnp.dot(jnp.concatenate([low, high, high], axis=1), matrix, preferred_element_type=f32)

    block = 512

    for step in range(PARTS * GROUP // block):
        rows = pl.ds(step * block, block)
        signal = product(left_ref[0, 0, rows, :], left_ref[0, 1, rows, :])
        taps = product(left_ref[1, 0, rows, :], left_ref[1, 1, rows, :])
        a, b = signal[:, :ROWS], signal[:, ROWS:]
        c, d = taps[:, :ROWS], taps[:, ROWS:]
        real, imag = split((a * c - b * d) * (1.0 / POINTS)), split((a * d + b * c) * (-1.0 / POINTS))
        high = jnp.concatenate([real[0], imag[0]], axis=1)
        low = jnp.concatenate([real[1], imag[1]], axis=1)
        back_ref[rows, :] = product(high, low)

    @pl.loop(0, GROUP // SLAB)
    def _(step):
        offset = pl.multiple_of(step * SLAB, SLAB)
        for m in range(4):
            values = []
            for p in range(8):
                j = 4 * p + m
                real = back_ref[rows_of(j, offset), :ROWS]
                imag = -back_ref[rows_of(j, offset), ROWS:]
                c, s = twists_ref[j, 0][None, :], twists_ref[j, 1][None, :]
                values.append((real * c - imag * s, real * s + imag * c))
            for a, value in enumerate(small_transform(values, 1)):
                real, imag = turned(value, a * (4 * m + 1) / 128)
                first_ref[m, a, 0] = real
                first_ref[m, a, 1] = imag
        skip = skip_ref[pl.ds(offset, SLAB), :]
        for a in range(8):
            values = [(first_ref[m, a, 0], first_ref[m, a, 1]) for m in range(4)]
            for q, (real, imag) in enumerate(small_transform(values, 1)):
                angle = 2.0 * math.pi * q / 16
                conv = real * math.cos(angle) - imag * math.sin(angle) if q else real
                s = a + 8 * q
                gated = gated_ref[s, pl.ds(offset, SLAB), :]
                out_ref[s, pl.ds(offset, SLAB), :] = (conv + skip * gated).astype(bf16)

    for _, _, copy in copies:
        copy.wait()


def fetch(weights_ref, target_ref, sems, away, me_ref, pieces, first=0):
    columns = (me_ref[0] + away) % RING * WIDE
    copies = []
    for i, (start, stop) in enumerate(pieces):
        source = weights_ref.at[:, pl.ds(pl.multiple_of(columns + start, 128), stop - start)]
        target = target_ref.at[:, start - first : stop - first]
        copies.append((start, stop, pltpu.make_async_copy(source, target, sems.at[i])))
        copies[-1][2].start()
    return copies


def part_of(rows_ref, held_ref, start, stop):
    return jnp.dot(rows_ref[...], held_ref[:, start:stop], preferred_element_type=f32)


def far_kernel(me_ref, outer_ref, query_ref, first_ref, weights_ref, up_ref, down_ref, rows_ref, held_ref, sems):
    copies = fetch(weights_ref, held_ref, sems, 2, me_ref, RIGHT, UP)
    rows_ref[...] = (query_ref[...] * outer_ref[...].T.astype(f32)).astype(bf16)
    for start, stop in LEFT:
        up_ref[:, start:stop] = part_of(rows_ref, first_ref, start, stop).astype(bf16)
    for start, stop, copy in copies:
        copy.wait()
        here = slice(start - UP, stop - UP)
        down_ref[:, here] = part_of(rows_ref, held_ref, start - UP, stop - UP).astype(bf16)


def near_kernel(me_ref, rows_ref, weights_ref, up_ref, down_ref, later_ref, held_ref, sems):
    right = fetch(weights_ref, held_ref, sems, 1, me_ref, RIGHT)
    left = fetch(weights_ref, held_ref, sems.at[len(RIGHT) :], -1, me_ref, LEFT)
    later = fetch(weights_ref, later_ref, sems.at[len(RIGHT) + len(LEFT) :], 1, me_ref, LEFT)
    for start, stop, copy in right:
        copy.wait()
        up_ref[:, start - UP : stop - UP] = part_of(rows_ref, held_ref, start, stop).astype(bf16)
    for start, stop, copy in left:
        copy.wait()
        down_ref[:, start:stop] = part_of(rows_ref, held_ref, start, stop).astype(bf16)
    for _, _, copy in later:
        copy.wait()


def adding_kernel(me_ref, rows_ref, first_ref, far_up_ref, far_down_ref, weights_ref, up_ref, down_ref, held_ref, sems):
    copies = fetch(weights_ref, held_ref, sems, -1, me_ref, RIGHT, UP)
    for start, stop in LEFT:
        total = part_of(rows_ref, first_ref, start, stop)
        up_ref[:, start:stop] = (total + far_up_ref[:, start:stop].astype(f32)).astype(bf16)
    for start, stop, copy in copies:
        copy.wait()
        here = slice(start - UP, stop - UP)
        total = part_of(rows_ref, held_ref, start - UP, stop - UP)
        down_ref[:, here] = (total + far_down_ref[:, here].astype(f32)).astype(bf16)


def own_kernel(me_ref, rows_ref, near_up_ref, near_down_ref, weights_ref, out_ref, held_ref, sems):
    for start, stop, copy in fetch(weights_ref, held_ref, sems, 0, me_ref, LEFT + RIGHT):
        copy.wait()
        arrived = near_down_ref[:, start:stop] if start < UP else near_up_ref[:, start - UP : stop - UP]
        out_ref[:, start:stop] = part_of(rows_ref, held_ref, start, stop) + arrived.astype(f32)


def last_kernel(own_ref, both_up_ref, both_down_ref, out_ref):
    for part, arrived_ref in ((slice(0, UP), both_up_ref), (slice(UP, WIDE), both_down_ref)):
        out_ref[:, part] = (own_ref[:, part] + arrived_ref[...].astype(f32)).astype(bf16)


RING = 4
WIDE = 2048
UP = 1024
LEFT = ((0, 512), (512, UP))
RIGHT = ((UP, 1536), (1536, WIDE))
SENT = 3
EDGE = 16
VMEM = pl.BlockSpec(memory_space=pltpu.VMEM)
SMEM = pl.BlockSpec(memory_space=pltpu.SMEM)
HBM = pl.BlockSpec(memory_space=pltpu.HBM)


def share(kernel, arrays, outs, held):
    return pl.pallas_call(
        kernel,
        in_specs=[SMEM] + [VMEM] * (len(arrays) - 2) + [HBM],
        out_specs=[VMEM] * len(outs),
        out_shape=[pltpu.VMEM(shape, dtype) for shape, dtype in outs],
        scratch_shapes=[
            pltpu.VMEM((arrays[-1].shape[0], held), bf16),
            pltpu.SemaphoreType.DMA((2 * len(LEFT) + len(RIGHT),)),
        ],
        cost_estimate=pl.CostEstimate(flops=2**31, bytes_accessed=2**21, transcendentals=0),
        compiler_params=pltpu.CompilerParams(vmem_limit_bytes=16 * 2**20),
    )(*arrays)


def project(me, outer, query, weights, held):
    up = [(i, (i + 1) % RING) for i in range(RING)]
    down = [(i, (i - 1) % RING) for i in range(RING)]
    left, right = ((ROWS, UP), bf16), ((ROWS, WIDE - UP), bf16)
    far_up, far_down, rows = share(
        far_kernel, (me, outer, query, held, weights), [left, right, (query.shape, bf16)], WIDE - UP
    )
    far_up = lax.ppermute(far_up, "ch", up)
    far_down = lax.ppermute(far_down, "ch", down)
    later = ((weights.shape[0], UP), bf16)
    near_up, near_down, later = share(near_kernel, (me, rows, weights), [right, left, later], WIDE)
    near_up = lax.ppermute(near_up, "ch", up)
    near_down = lax.ppermute(near_down, "ch", down)
    both_up, both_down = share(
        adding_kernel, (me, rows, later, far_up, far_down, weights), [left, right], WIDE - UP
    )
    both_up = lax.ppermute(both_up, "ch", up)
    both_down = lax.ppermute(both_down, "ch", down)
    (own,) = share(own_kernel, (me, rows, near_up, near_down, weights), [((ROWS, WIDE), f32)], WIDE)
    return pl.pallas_call(
        last_kernel,
        in_specs=[VMEM] * 3,
        out_specs=VMEM,
        out_shape=jax.ShapeDtypeStruct((ROWS, WIDE), bf16),
        compiler_params=pltpu.CompilerParams(vmem_limit_bytes=16 * 2**20),
    )(own, both_up, both_down)


def stage(after, *arrays):
    arrays = [pltpu.with_memory_space_constraint(array, pltpu.HBM) for array in arrays]
    return pl.pallas_call(
        stage_kernel,
        in_specs=[pl.BlockSpec(memory_space=pl.ANY)] + [HBM] * len(arrays),
        out_specs=[VMEM] * len(arrays),
        out_shape=[pltpu.VMEM(array.shape, array.dtype) for array in arrays],
        scratch_shapes=[pltpu.SemaphoreType.DMA((len(arrays),))],
        compiler_params=pltpu.CompilerParams(vmem_limit_bytes=16 * 2**20),
    )(after, *arrays)


def convolve(*arrays):
    channels = arrays[-1].shape[0]
    return pl.pallas_call(
        conv_kernel,
        in_specs=[SMEM] + [VMEM] * 6 + [HBM],
        out_specs=[VMEM, VMEM],
        out_shape=[
            pltpu.VMEM((PARTS, GROUP, ROWS), bf16),
            pltpu.VMEM((channels, UP), bf16),
        ],
        scratch_shapes=[
            pltpu.VMEM((PARTS, GROUP, ROWS), f32),
            pltpu.VMEM((4, 8, 2, SLAB, ROWS), f32),
            pltpu.VMEM((2, 2, PARTS * GROUP, 2 * ROWS), bf16),
            pltpu.VMEM((PARTS * GROUP, 2 * ROWS), f32),
            pltpu.SemaphoreType.DMA((len(LEFT),)),
        ],
        compiler_params=pltpu.CompilerParams(vmem_limit_bytes=16 * 2**20),
    )(*arrays)


def on_device(streams, short_taps, long_filter, skip_gain, out_weights):
    channels = streams.shape[2]
    streams = pltpu.with_memory_space_constraint(streams, pltpu.HBM)
    weights = pltpu.with_memory_space_constraint(out_weights, pltpu.HBM)
    me = lax.axis_index("ch").astype(jnp.int32).reshape(1)
    packed, edge = pl.pallas_call(
        exchange_kernel,
        in_specs=[HBM, HBM],
        out_specs=[VMEM, VMEM],
        out_shape=[
            pltpu.VMEM((PARTS, SENT * GROUP, ROWS), bf16),
            pltpu.VMEM((EDGE, channels), bf16),
        ],
        scratch_shapes=[
            pltpu.VMEM((SENT - 1, ROWS, channels), bf16),
            pltpu.VMEM((ROWS, channels), f32),
            pltpu.SemaphoreType.DMA((SENT + 1,)),
        ],
        compiler_params=pltpu.CompilerParams(vmem_limit_bytes=8 * 2**20),
    )(streams, pltpu.with_memory_space_constraint(long_filter, pltpu.HBM))
    high, low, twists = (jnp.asarray(table) for table in tables())
    high, low, twists, short_taps = stage(edge, high, low, twists, short_taps)
    arrived = lax.all_to_all(packed, "seq", 0, 0, tiled=True)
    edge = lax.ppermute(edge, "seq", [(i, i + 1) for i in range(PARTS - 1)])
    first = lax.axis_index("seq") * GROUP
    taps = lax.dynamic_slice_in_dim(short_taps[1:].reshape((SENT - 1) * SHORT, channels), first, GROUP, 1)
    taps = jnp.broadcast_to(taps[:, :, None], ((SENT - 1) * SHORT, GROUP, ROWS))
    skip = jnp.broadcast_to(lax.dynamic_slice_in_dim(skip_gain, first, GROUP, 0)[:, None], (GROUP, ROWS))
    outer, held = convolve(me, arrived, taps, skip, high, low, twists, weights)
    query = pl.pallas_call(
        query_kernel,
        in_specs=[HBM, VMEM, VMEM, VMEM],
        out_specs=VMEM,
        out_shape=pltpu.VMEM((ROWS, channels), f32),
        scratch_shapes=[pltpu.VMEM((ROWS, channels), bf16), pltpu.SemaphoreType.DMA((1,))],
        compiler_params=pltpu.CompilerParams(vmem_limit_bytes=8 * 2**20),
    )(streams, edge, short_taps, held)
    outer = lax.all_to_all(outer, "seq", 0, 0, tiled=True)
    return project(me, outer.reshape(channels, ROWS), query, weights, held)


def solution(mesh):
    return jax.shard_map(
        on_device,
        mesh=mesh,
        in_specs=(
            P(None, "seq", "ch"),
            P(None, None, "ch"),
            P("seq", "ch"),
            P("ch"),
            P("ch", None),
        ),
        out_specs=P("seq", "ch"),
        check_vma=False,
    )
```

```python
import functools
import math

import jax
import jax.numpy as jnp
import numpy as np
from jax import lax
from jax.experimental import pallas as pl
from jax.experimental.pallas import tpu as pltpu
from jax.sharding import PartitionSpec as P

SHORT = 3
ROWS = 128
PARTS = 32
GROUP = 32
SLAB = 16
POINTS = PARTS * ROWS
f32 = jnp.float32
bf16 = jnp.bfloat16


def tables():
    r = np.arange(ROWS)
    angle = 2.0 * np.pi * (np.outer(r, r) % ROWS) / ROWS
    cosine, sine = np.cos(angle), np.sin(angle)
    matrix = np.block([[cosine, -sine], [sine, cosine]])
    high = matrix.astype(np.float32).astype(bf16)
    low = (matrix - high.astype(np.float64)).astype(np.float32).astype(bf16)
    j = np.arange(PARTS)
    twist = 2.0 * np.pi * np.outer(4 * j + 1, r) / (4 * POINTS)
    twists = np.stack([np.cos(twist), np.sin(twist)], axis=1).astype(np.float32)
    return high, low, twists


def turned(value, turns):
    real, imag = value
    eighth = turns * 8 % 8
    if eighth == 0:
        return real, imag
    if eighth == 2:
        return -imag, real
    if eighth == 4:
        return -real, -imag
    if eighth == 6:
        return imag, -real
    if eighth in (1, 3, 5, 7):
        half = math.sqrt(0.5)
        total, apart = (real + imag) * half, (real - imag) * half
        return {1: (apart, total), 3: (-total, apart), 5: (-apart, -total), 7: (total, -apart)}[int(eighth)]
    c, s = math.cos(2.0 * math.pi * turns), math.sin(2.0 * math.pi * turns)
    return real * c - imag * s, real * s + imag * c


def plus(a, b):
    return a[0] + b[0], a[1] + b[1]


def minus(a, b):
    return a[0] - b[0], a[1] - b[1]


def small_transform(values, sign):
    count = len(values)
    if count == 1:
        return values
    even = small_transform(values[0::2], sign)
    odd = small_transform(values[1::2], sign)
    odd = [turned(value, sign * k / count) for k, value in enumerate(odd)]
    return [plus(a, b) for a, b in zip(even, odd)] + [minus(a, b) for a, b in zip(even, odd)]


def exchange_kernel(streams_ref, filter_ref, out_ref, edge_ref, rows_ref, taps_ref, sems):
    copies = [pltpu.make_async_copy(streams_ref.at[i + 1], rows_ref.at[i], sems.at[i]) for i in range(SENT - 1)]
    copies.append(pltpu.make_async_copy(filter_ref, taps_ref, sems.at[SENT - 1]))
    edge = pltpu.make_async_copy(streams_ref.at[0, ROWS - EDGE :], edge_ref, sems.at[SENT])
    for copy in copies:
        copy.start()
    edge.start()
    wide = 8 * GROUP
    for j, copy in enumerate(copies):
        copy.wait()
        for first in range(0, PARTS * GROUP, wide):
            here = slice(first, first + wide)
            block = rows_ref[j, :, here] if j < SENT - 1 else taps_ref[:, here].astype(bf16)
            parts = pl.ds(first // GROUP, wide // GROUP)
            out_ref[parts, j * GROUP : (j + 1) * GROUP, :] = block.T.reshape(wide // GROUP, GROUP, ROWS)
    edge.wait()


def stage_kernel(*refs):
    sems, bounce_ref = refs[-1], refs[-2]
    tables_in, weights_ref = refs[1 : 1 + TABLES], refs[1 + TABLES]
    tables_out = refs[2 + TABLES : 2 + 2 * TABLES]
    rest_ref, near_ref, later_ref = refs[-5:-2]
    copies = [
        pltpu.make_async_copy(source, target, sems.at[i]) for i, (source, target) in enumerate(zip(tables_in, tables_out))
    ]
    for copy in copies:
        copy.start()
    count, arriving = TABLES, []
    for target_ref, at, away, pieces, first in (
        (near_ref, 0, 1, RIGHT, 0), (near_ref, 0, RING - 1, LEFT, 0), (rest_ref, WIDE, 2, RIGHT, UP),
        (later_ref, 2 * WIDE - UP, 1, LEFT, 0), (later_ref, 2 * WIDE - UP, RING - 1, RIGHT, 0),
    ):
        held_ref = bounce_ref.at[:, at : at + target_ref.shape[1]]
        for start, stop, copy in fetch(weights_ref, held_ref, sems.at[count:], away, pieces, first):
            here = slice(start - first, stop - first)
            arriving.append((copy, pltpu.make_async_copy(held_ref.at[:, here], target_ref.at[:, here], sems.at[count])))
            count += 1
    for copy, onward in arriving:
        copy.wait()
        onward.start()
        copies.append(onward)
    for copy in copies:
        copy.wait()


def query_kernel(streams_ref, edge_ref, taps_ref, held_ref, out_ref, rows_ref, sem):
    copy = pltpu.make_async_copy(streams_ref.at[0], rows_ref, sem.at[0])
    copy.start()
    copy.wait()
    now = rows_ref[...].astype(f32)
    earlier = edge_ref[...].astype(f32)
    row = lax.broadcasted_iota(jnp.int32, now.shape, 0)
    last, before_last = earlier[EDGE - 1 :, :], earlier[EDGE - 2 : EDGE - 1, :]
    one = jnp.where(row == 0, last, pltpu.roll(now, 1, 0))
    two = jnp.where(row == 0, before_last, jnp.where(row == 1, last, pltpu.roll(now, 2, 0)))
    out_ref[...] = taps_ref[0, 0:1, :] * now + taps_ref[0, 1:2, :] * one + taps_ref[0, 2:3, :] * two


def split(value):
    high = value.astype(bf16)
    return high, (value - high.astype(f32)).astype(bf16)


def conv_kernel(
    x_ref, taps_ref, skip_ref, high_ref, low_ref, twists_ref, weights_ref,
    out_ref, held_ref, gated_ref, first_ref, left_ref, back_ref, sems,
):
    copies = fetch(weights_ref, held_ref, sems, 2, LEFT)
    lane = lax.broadcasted_iota(jnp.int32, (SLAB, ROWS), 1)

    def rows_of(j, offset):
        return pl.ds(pl.multiple_of(j * GROUP + offset, SLAB), SLAB)

    def short(stream, offset):
        taps = [taps_ref[stream * SHORT + i, pl.ds(offset, SLAB), :] for i in range(SHORT)]
        before = [jnp.zeros((SLAB, ROWS), f32)] * 2
        for s in range(PARTS):
            now = x_ref[s, rows_of(stream, offset), :].astype(f32)
            moved = [pltpu.roll(now, i, 1) for i in (1, 2)]
            total = taps[0] * now
            for i in (1, 2):
                total = total + taps[i] * jnp.where(lane < i, before[i - 1], moved[i - 1])
            before = moved
            yield total

    def forward(slot, offset, load):
        for a in range(8):
            values = []
            for q in range(4):
                value = load(a + 8 * q)
                angle = -2.0 * math.pi * q / 16
                values.append((value * math.cos(angle), value * math.sin(angle)) if q else (value, jnp.zeros_like(value)))
            for m, value in enumerate(small_transform(values, -1)):
                real, imag = turned(value, -a * (4 * m + 1) / 128)
                first_ref[m, a, 0] = real
                first_ref[m, a, 1] = imag
        for m in range(4):
            values = [(first_ref[m, a, 0], first_ref[m, a, 1]) for a in range(8)]
            for p, (real, imag) in enumerate(small_transform(values, -1)):
                j = 4 * p + m
                c, s = twists_ref[j, 0][None, :], twists_ref[j, 1][None, :]
                for half, part in enumerate((real * c + imag * s, imag * c - real * s)):
                    high, low = split(part)
                    left_ref[slot, 0, rows_of(j, offset), half * ROWS : (half + 1) * ROWS] = high
                    left_ref[slot, 1, rows_of(j, offset), half * ROWS : (half + 1) * ROWS] = low

    @pl.loop(0, GROUP // SLAB)
    def _(step):
        offset = pl.multiple_of(step * SLAB, SLAB)
        for s, (key, value) in enumerate(zip(short(0, offset), short(1, offset))):
            gated_ref[s, pl.ds(offset, SLAB), :] = key * value
        forward(0, offset, lambda s: gated_ref[s, pl.ds(offset, SLAB), :])
        forward(1, offset, lambda s: x_ref[s, rows_of(SENT - 1, offset), :].astype(f32))

    matrix = jnp.concatenate([high_ref[...], low_ref[...], high_ref[...]], axis=0)

    def product(high, low):
        return jnp.dot(jnp.concatenate([low, high, high], axis=1), matrix, preferred_element_type=f32)

    block = 256
    blocks = [pl.ds(start, block) for start in range(0, PARTS * GROUP, block)]
    for rows in blocks:
        signal = product(left_ref[0, 0, rows, :], left_ref[0, 1, rows, :])
        taps = product(left_ref[1, 0, rows, :], left_ref[1, 1, rows, :])
        a, b = signal[:, :ROWS], signal[:, ROWS:]
        c, d = taps[:, :ROWS], taps[:, ROWS:]
        real, imag = split((a * c - b * d) * (1.0 / POINTS)), split((a * d + b * c) * (-1.0 / POINTS))
        left_ref[0, 0, rows, :] = jnp.concatenate([real[0], imag[0]], axis=1)
        left_ref[0, 1, rows, :] = jnp.concatenate([real[1], imag[1]], axis=1)
    for rows in blocks:
        back_ref[rows, :] = product(left_ref[0, 0, rows, :], left_ref[0, 1, rows, :])

    @pl.loop(0, GROUP // SLAB)
    def _(step):
        offset = pl.multiple_of(step * SLAB, SLAB)
        for m in range(4):
            values = []
            for p in range(8):
                j = 4 * p + m
                real = back_ref[rows_of(j, offset), :ROWS]
                imag = -back_ref[rows_of(j, offset), ROWS:]
                c, s = twists_ref[j, 0][None, :], twists_ref[j, 1][None, :]
                values.append((real * c - imag * s, real * s + imag * c))
            for a, value in enumerate(small_transform(values, 1)):
                real, imag = turned(value, a * (4 * m + 1) / 128)
                first_ref[m, a, 0] = real
                first_ref[m, a, 1] = imag
        skip = skip_ref[pl.ds(offset, SLAB), :]
        for a in range(8):
            values = [(first_ref[m, a, 0], first_ref[m, a, 1]) for m in range(4)]
            for q, (real, imag) in enumerate(small_transform(values, 1)):
                angle = 2.0 * math.pi * q / 16
                conv = real * math.cos(angle) - imag * math.sin(angle) if q else real
                s = a + 8 * q
                gated = gated_ref[s, pl.ds(offset, SLAB), :]
                out_ref[s, pl.ds(offset, SLAB), :] = (conv + skip * gated).astype(bf16)

    for _, _, copy in copies:
        copy.wait()


def fetch(weights_ref, target_ref, sems, away, pieces, first=0):
    columns = (lax.axis_index("ch") + away) % RING * WIDE
    copies = []
    for i, (start, stop) in enumerate(pieces):
        source = weights_ref.at[:, pl.ds(pl.multiple_of(columns + start, 128), stop - start)]
        target = target_ref.at[:, start - first : stop - first]
        copies.append((start, stop, pltpu.make_async_copy(source, target, sems.at[i])))
        copies[-1][2].start()
    return copies


def part_of(rows_ref, held_ref, start, stop):
    return jnp.dot(rows_ref[...], held_ref[:, start:stop], preferred_element_type=f32)


def mixing_kernel(outer_ref, query_ref, held_ref, up_ref, rows_ref):
    rows_ref[...] = (query_ref[...] * outer_ref[...].T.astype(f32)).astype(bf16)
    for start, stop in LEFT:
        up_ref[:, start:stop] = part_of(rows_ref, held_ref, start, stop).astype(bf16)


def far_kernel(rows_ref, rest_ref, down_ref):
    for start, stop in RIGHT:
        down_ref[:, start - UP : stop - UP] = part_of(rows_ref, rest_ref, start - UP, stop - UP).astype(bf16)


def near_kernel(rows_ref, near_ref, up_ref, down_ref):
    for start, stop in RIGHT:
        up_ref[:, start - UP : stop - UP] = part_of(rows_ref, near_ref, start, stop).astype(bf16)
    for start, stop in LEFT:
        down_ref[:, start:stop] = part_of(rows_ref, near_ref, start, stop).astype(bf16)


def adding_kernel(rows_ref, later_ref, far_up_ref, far_down_ref, up_ref, down_ref):
    for start, stop in LEFT:
        total = part_of(rows_ref, later_ref, start, stop)
        up_ref[:, start:stop] = (total + far_up_ref[:, start:stop].astype(f32)).astype(bf16)
    for start, stop in RIGHT:
        here = slice(start - UP, stop - UP)
        total = part_of(rows_ref, later_ref, start, stop)
        down_ref[:, here] = (total + far_down_ref[:, here].astype(f32)).astype(bf16)


def own_kernel(rows_ref, near_up_ref, near_down_ref, weights_ref, out_ref, held_ref, sems):
    for start, stop, copy in fetch(weights_ref, held_ref, sems, 0, LEFT + RIGHT):
        copy.wait()
        arrived = near_down_ref[:, start:stop] if start < UP else near_up_ref[:, start - UP : stop - UP]
        out_ref[:, start:stop] = part_of(rows_ref, held_ref, start, stop) + arrived.astype(f32)


def last_kernel(own_ref, both_up_ref, both_down_ref, out_ref):
    for part, arrived_ref in ((slice(0, UP), both_up_ref), (slice(UP, WIDE), both_down_ref)):
        out_ref[:, part] = (own_ref[:, part] + arrived_ref[...].astype(f32)).astype(bf16)


TABLES = 4
RING = 4
WIDE = 2048
UP = 1024
LEFT = ((0, 512), (512, UP))
RIGHT = ((UP, 1536), (1536, WIDE))
SENT = 3
EDGE = 16
VMEM = pl.BlockSpec(memory_space=pltpu.VMEM)
HBM = pl.BlockSpec(memory_space=pltpu.HBM)


def share(kernel, arrays, outs, held):
    return pl.pallas_call(
        kernel,
        in_specs=[VMEM] * (len(arrays) - 1) + [HBM],
        out_specs=[VMEM] * len(outs),
        out_shape=[pltpu.VMEM(shape, dtype) for shape, dtype in outs],
        scratch_shapes=[
            pltpu.VMEM((arrays[-1].shape[0], held), bf16),
            pltpu.SemaphoreType.DMA((2 * len(LEFT) + len(RIGHT),)),
        ],
        cost_estimate=pl.CostEstimate(flops=2**31, bytes_accessed=2**21, transcendentals=0),
        compiler_params=pltpu.CompilerParams(vmem_limit_bytes=16 * 2**20),
    )(*arrays)


def plain(kernel, arrays, outs):
    return pl.pallas_call(
        kernel,
        in_specs=[VMEM] * len(arrays),
        out_specs=[VMEM] * len(outs),
        out_shape=[pltpu.VMEM(shape, dtype) for shape, dtype in outs],
        cost_estimate=pl.CostEstimate(flops=2**31, bytes_accessed=2**21, transcendentals=0),
        compiler_params=pltpu.CompilerParams(vmem_limit_bytes=8 * 2**20),
    )(*arrays)


def project(outer, query, weights, held, rest, near, later):
    up = [(i, (i + 1) % RING) for i in range(RING)]
    down = [(i, (i - 1) % RING) for i in range(RING)]
    left, right = ((ROWS, UP), bf16), ((ROWS, WIDE - UP), bf16)
    far_up, rows = plain(mixing_kernel, (outer, query, held), [left, (query.shape, bf16)])
    far_up = lax.ppermute(far_up, "ch", up)
    (far_down,) = plain(far_kernel, (rows, rest), [right])
    far_down = lax.ppermute(far_down, "ch", down)
    near_up, near_down = plain(near_kernel, (rows, near), [right, left])
    near_up = lax.ppermute(near_up, "ch", up)
    near_down = lax.ppermute(near_down, "ch", down)
    both_up, both_down = plain(adding_kernel, (rows, later, far_up, far_down), [left, right])
    both_up = lax.ppermute(both_up, "ch", up)
    both_down = lax.ppermute(both_down, "ch", down)
    (own,) = share(own_kernel, (rows, near_up, near_down, weights), [((ROWS, WIDE), f32)], WIDE)
    return pl.pallas_call(
        last_kernel,
        in_specs=[VMEM] * 3,
        out_specs=VMEM,
        out_shape=jax.ShapeDtypeStruct((ROWS, WIDE), bf16),
        compiler_params=pltpu.CompilerParams(vmem_limit_bytes=16 * 2**20),
    )(own, both_up, both_down)


def stage(after, weights, *arrays):
    arrays = [pltpu.with_memory_space_constraint(array, pltpu.HBM) for array in arrays]
    parts = [pltpu.HBM((weights.shape[0], wide), bf16) for wide in (WIDE - UP, WIDE, WIDE)]
    return pl.pallas_call(
        stage_kernel,
        in_specs=[pl.BlockSpec(memory_space=pl.ANY)] + [HBM] * (len(arrays) + 1),
        out_specs=[VMEM] * len(arrays) + [HBM] * len(parts),
        out_shape=[pltpu.VMEM(array.shape, array.dtype) for array in arrays] + parts,
        scratch_shapes=[
            pltpu.VMEM((weights.shape[0], 3 * WIDE - UP), bf16),
            pltpu.SemaphoreType.DMA((len(arrays) + 2 * len(LEFT) + 3 * len(RIGHT),)),
        ],
        compiler_params=pltpu.CompilerParams(vmem_limit_bytes=16 * 2**20),
    )(after, *arrays, weights)


def convolve(*arrays):
    channels = arrays[-1].shape[0]
    return pl.pallas_call(
        conv_kernel,
        in_specs=[VMEM] * 6 + [HBM],
        out_specs=[VMEM, VMEM],
        out_shape=[
            pltpu.VMEM((PARTS, GROUP, ROWS), bf16),
            pltpu.VMEM((channels, UP), bf16),
        ],
        scratch_shapes=[
            pltpu.VMEM((PARTS, GROUP, ROWS), f32),
            pltpu.VMEM((4, 8, 2, SLAB, ROWS), f32),
            pltpu.VMEM((2, 2, PARTS * GROUP, 2 * ROWS), bf16),
            pltpu.VMEM((PARTS * GROUP, 2 * ROWS), f32),
            pltpu.SemaphoreType.DMA((len(LEFT),)),
        ],
        compiler_params=pltpu.CompilerParams(vmem_limit_bytes=16 * 2**20),
    )(*arrays)


def on_device(streams, short_taps, long_filter, skip_gain, out_weights):
    channels = streams.shape[2]
    streams = pltpu.with_memory_space_constraint(streams, pltpu.HBM)
    weights = pltpu.with_memory_space_constraint(out_weights, pltpu.HBM)
    packed, edge = pl.pallas_call(
        exchange_kernel,
        in_specs=[HBM, HBM],
        out_specs=[VMEM, VMEM],
        out_shape=[
            pltpu.VMEM((PARTS, SENT * GROUP, ROWS), bf16),
            pltpu.VMEM((EDGE, channels), bf16),
        ],
        scratch_shapes=[
            pltpu.VMEM((SENT - 1, ROWS, channels), bf16),
            pltpu.VMEM((ROWS, channels), f32),
            pltpu.SemaphoreType.DMA((SENT + 1,)),
        ],
        compiler_params=pltpu.CompilerParams(vmem_limit_bytes=8 * 2**20),
    )(streams, pltpu.with_memory_space_constraint(long_filter, pltpu.HBM))
    high, low, twists = (jnp.asarray(table) for table in tables())
    high, low, twists, short_taps, *parts = stage(edge, weights, high, low, twists, short_taps)
    arrived = lax.all_to_all(packed, "seq", 0, 0, tiled=True)
    edge = lax.ppermute(edge, "seq", [(i, i + 1) for i in range(PARTS - 1)])
    first = lax.axis_index("seq") * GROUP
    taps = lax.dynamic_slice_in_dim(short_taps[1:].reshape((SENT - 1) * SHORT, channels), first, GROUP, 1)
    taps = jnp.broadcast_to(taps[:, :, None], ((SENT - 1) * SHORT, GROUP, ROWS))
    skip = jnp.broadcast_to(lax.dynamic_slice_in_dim(skip_gain, first, GROUP, 0)[:, None], (GROUP, ROWS))
    outer, held = convolve(arrived, taps, skip, high, low, twists, weights)
    query = pl.pallas_call(
        query_kernel,
        in_specs=[HBM, VMEM, VMEM, VMEM],
        out_specs=VMEM,
        out_shape=pltpu.VMEM((ROWS, channels), f32),
        scratch_shapes=[pltpu.VMEM((ROWS, channels), bf16), pltpu.SemaphoreType.DMA((1,))],
        compiler_params=pltpu.CompilerParams(vmem_limit_bytes=8 * 2**20),
    )(streams, edge, short_taps, held)
    outer = lax.all_to_all(outer, "seq", 0, 0, tiled=True)
    return project(outer.reshape(channels, ROWS), query, weights, held, *parts)


def solution(mesh):
    return jax.shard_map(
        on_device,
        mesh=mesh,
        in_specs=(
            P(None, "seq", "ch"),
            P(None, None, "ch"),
            P("seq", "ch"),
            P("ch"),
            P("ch", None),
        ),
        out_specs=P("seq", "ch"),
        check_vma=False,
    )
```

```python
import functools
import math

import jax
import jax.numpy as jnp
import numpy as np
from jax import lax
from jax.experimental import pallas as pl
from jax.experimental.pallas import tpu as pltpu
from jax.sharding import PartitionSpec as P

SHORT = 3
ROWS = 128
PARTS = 32
GROUP = 32
SLAB = 16
POINTS = PARTS * ROWS
f32 = jnp.float32
bf16 = jnp.bfloat16


def tables():
    r = np.arange(ROWS)
    angle = 2.0 * np.pi * (np.outer(r, r) % ROWS) / ROWS
    cosine, sine = np.cos(angle), np.sin(angle)
    matrix = np.block([[cosine, -sine], [sine, cosine]])
    high = matrix.astype(np.float32).astype(bf16)
    low = (matrix - high.astype(np.float64)).astype(np.float32).astype(bf16)
    j = np.arange(PARTS)
    twist = 2.0 * np.pi * np.outer(4 * j + 1, r) / (4 * POINTS)
    twists = np.stack([np.cos(twist), np.sin(twist)], axis=1).astype(np.float32)
    return high, low, twists


def turned(value, turns):
    real, imag = value
    eighth = turns * 8 % 8
    if eighth == 0:
        return real, imag
    if eighth == 2:
        return -imag, real
    if eighth == 4:
        return -real, -imag
    if eighth == 6:
        return imag, -real
    if eighth in (1, 3, 5, 7):
        half = math.sqrt(0.5)
        total, apart = (real + imag) * half, (real - imag) * half
        return {1: (apart, total), 3: (-total, apart), 5: (-apart, -total), 7: (total, -apart)}[int(eighth)]
    c, s = math.cos(2.0 * math.pi * turns), math.sin(2.0 * math.pi * turns)
    return real * c - imag * s, real * s + imag * c


def plus(a, b):
    return a[0] + b[0], a[1] + b[1]


def minus(a, b):
    return a[0] - b[0], a[1] - b[1]


def small_transform(values, sign):
    count = len(values)
    if count == 1:
        return values
    even = small_transform(values[0::2], sign)
    odd = small_transform(values[1::2], sign)
    odd = [turned(value, sign * k / count) for k, value in enumerate(odd)]
    return [plus(a, b) for a, b in zip(even, odd)] + [minus(a, b) for a, b in zip(even, odd)]


def exchange_kernel(streams_ref, filter_ref, out_ref, edge_ref, rows_ref, taps_ref, sems):
    copies = [pltpu.make_async_copy(streams_ref.at[i + 1], rows_ref.at[i], sems.at[i]) for i in range(SENT - 1)]
    copies.append(pltpu.make_async_copy(filter_ref, taps_ref, sems.at[SENT - 1]))
    edge = pltpu.make_async_copy(streams_ref.at[0, ROWS - EDGE :], edge_ref, sems.at[SENT])
    for copy in copies:
        copy.start()
    edge.start()
    wide = 8 * GROUP
    for j, copy in enumerate(copies):
        copy.wait()
        for first in range(0, PARTS * GROUP, wide):
            here = slice(first, first + wide)
            block = rows_ref[j, :, here] if j < SENT - 1 else taps_ref[:, here].astype(bf16)
            parts = pl.ds(first // GROUP, wide // GROUP)
            out_ref[parts, j * GROUP : (j + 1) * GROUP, :] = block.T.reshape(wide // GROUP, GROUP, ROWS)
    edge.wait()


def stage_kernel(*refs):
    sems, bounce_ref = refs[-1], refs[-2]
    tables_in, weights_ref = refs[1 : 1 + TABLES], refs[1 + TABLES]
    tables_out = refs[2 + TABLES : 2 + 2 * TABLES]
    rest_ref, near_ref, later_ref = refs[-5:-2]
    copies = [
        pltpu.make_async_copy(source, target, sems.at[i]) for i, (source, target) in enumerate(zip(tables_in, tables_out))
    ]
    for copy in copies:
        copy.start()
    count, arriving = TABLES, []
    for target_ref, at, away, pieces, first in (
        (near_ref, 0, 1, RIGHT, 0), (near_ref, 0, RING - 1, LEFT, 0), (rest_ref, WIDE, 2, RIGHT, UP),
        (later_ref, 2 * WIDE - UP, 1, LEFT, 0), (later_ref, 2 * WIDE - UP, RING - 1, RIGHT, 0),
    ):
        held_ref = bounce_ref.at[:, at : at + target_ref.shape[1]]
        for start, stop, copy in fetch(weights_ref, held_ref, sems.at[count:], away, pieces, first):
            here = slice(start - first, stop - first)
            arriving.append((copy, pltpu.make_async_copy(held_ref.at[:, here], target_ref.at[:, here], sems.at[count])))
            count += 1
    for copy, onward in arriving:
        copy.wait()
        onward.start()
        copies.append(onward)
    for copy in copies:
        copy.wait()


def query_kernel(streams_ref, edge_ref, taps_ref, held_ref, out_ref, rows_ref, sem):
    copy = pltpu.make_async_copy(streams_ref.at[0], rows_ref, sem.at[0])
    copy.start()
    copy.wait()
    now = rows_ref[...].astype(f32)
    earlier = edge_ref[...].astype(f32)
    row = lax.broadcasted_iota(jnp.int32, now.shape, 0)
    last, before_last = earlier[EDGE - 1 :, :], earlier[EDGE - 2 : EDGE - 1, :]
    one = jnp.where(row == 0, last, pltpu.roll(now, 1, 0))
    two = jnp.where(row == 0, before_last, jnp.where(row == 1, last, pltpu.roll(now, 2, 0)))
    out_ref[...] = taps_ref[0, 0:1, :] * now + taps_ref[0, 1:2, :] * one + taps_ref[0, 2:3, :] * two


def split(value):
    high = value.astype(bf16)
    return high, (value - high.astype(f32)).astype(bf16)


def conv_kernel(
    x_ref, taps_ref, skip_ref, high_ref, low_ref, twists_ref, weights_ref,
    out_ref, held_ref, gated_ref, first_ref, left_ref, back_ref, sems,
):
    copies = fetch(weights_ref, held_ref, sems, 2, LEFT)
    lane = lax.broadcasted_iota(jnp.int32, (SLAB, ROWS), 1)

    def rows_of(j, offset):
        return pl.ds(pl.multiple_of(j * GROUP + offset, SLAB), SLAB)

    def short(stream, offset):
        taps = [taps_ref[stream * SHORT + i, pl.ds(offset, SLAB), :] for i in range(SHORT)]
        before = [jnp.zeros((SLAB, ROWS), f32)] * 2
        for s in range(PARTS):
            now = x_ref[s, rows_of(stream, offset), :].astype(f32)
            moved = [pltpu.roll(now, i, 1) for i in (1, 2)]
            total = taps[0] * now
            for i in (1, 2):
                total = total + taps[i] * jnp.where(lane < i, before[i - 1], moved[i - 1])
            before = moved
            yield total

    def forward(slot, offset, load):
        for a in range(8):
            values = []
            for q in range(4):
                value = load(a + 8 * q)
                angle = -2.0 * math.pi * q / 16
                values.append((value * math.cos(angle), value * math.sin(angle)) if q else (value, jnp.zeros_like(value)))
            for m, value in enumerate(small_transform(values, -1)):
                real, imag = turned(value, -a * (4 * m + 1) / 128)
                first_ref[m, a, 0] = real
                first_ref[m, a, 1] = imag
        for m in range(4):
            values = [(first_ref[m, a, 0], first_ref[m, a, 1]) for a in range(8)]
            for p, (real, imag) in enumerate(small_transform(values, -1)):
                j = 4 * p + m
                c, s = twists_ref[j, 0][None, :], twists_ref[j, 1][None, :]
                for half, part in enumerate((real * c + imag * s, imag * c - real * s)):
                    high, low = split(part)
                    left_ref[slot, 0, rows_of(j, offset), half * ROWS : (half + 1) * ROWS] = high
                    left_ref[slot, 1, rows_of(j, offset), half * ROWS : (half + 1) * ROWS] = low

    @pl.loop(0, GROUP // SLAB)
    def _(step):
        offset = pl.multiple_of(step * SLAB, SLAB)
        for s, (key, value) in enumerate(zip(short(0, offset), short(1, offset))):
            gated_ref[s, pl.ds(offset, SLAB), :] = key * value
        forward(0, offset, lambda s: gated_ref[s, pl.ds(offset, SLAB), :])
        forward(1, offset, lambda s: x_ref[s, rows_of(SENT - 1, offset), :].astype(f32))

    matrix = jnp.concatenate([high_ref[...], low_ref[...], high_ref[...]], axis=0)

    def product(high, low):
        return jnp.dot(jnp.concatenate([low, high, high], axis=1), matrix, preferred_element_type=f32)

    block = 256
    blocks = [pl.ds(start, block) for start in range(0, PARTS * GROUP, block)]
    for rows in blocks:
        signal = product(left_ref[0, 0, rows, :], left_ref[0, 1, rows, :])
        taps = product(left_ref[1, 0, rows, :], left_ref[1, 1, rows, :])
        a, b = signal[:, :ROWS], signal[:, ROWS:]
        c, d = taps[:, :ROWS], taps[:, ROWS:]
        real, imag = split((a * c - b * d) * (1.0 / POINTS)), split((a * d + b * c) * (-1.0 / POINTS))
        left_ref[0, 0, rows, :] = jnp.concatenate([real[0], imag[0]], axis=1)
        left_ref[0, 1, rows, :] = jnp.concatenate([real[1], imag[1]], axis=1)
    for rows in blocks:
        back_ref[rows, :] = product(left_ref[0, 0, rows, :], left_ref[0, 1, rows, :])

    @pl.loop(0, GROUP // SLAB)
    def _(step):
        offset = pl.multiple_of(step * SLAB, SLAB)
        for m in range(4):
            values = []
            for p in range(8):
                j = 4 * p + m
                real = back_ref[rows_of(j, offset), :ROWS]
                imag = -back_ref[rows_of(j, offset), ROWS:]
                c, s = twists_ref[j, 0][None, :], twists_ref[j, 1][None, :]
                values.append((real * c - imag * s, real * s + imag * c))
            for a, value in enumerate(small_transform(values, 1)):
                real, imag = turned(value, a * (4 * m + 1) / 128)
                first_ref[m, a, 0] = real
                first_ref[m, a, 1] = imag
        skip = skip_ref[pl.ds(offset, SLAB), :]
        for a in range(8):
            values = [(first_ref[m, a, 0], first_ref[m, a, 1]) for m in range(4)]
            for q, (real, imag) in enumerate(small_transform(values, 1)):
                angle = 2.0 * math.pi * q / 16
                conv = real * math.cos(angle) - imag * math.sin(angle) if q else real
                s = a + 8 * q
                gated = gated_ref[s, pl.ds(offset, SLAB), :]
                out_ref[s, pl.ds(offset, SLAB), :] = (conv + skip * gated).astype(bf16)

    for _, _, copy in copies:
        copy.wait()


def fetch(weights_ref, target_ref, sems, away, pieces, first=0):
    columns = (lax.axis_index("ch") + away) % RING * WIDE
    copies = []
    for i, (start, stop) in enumerate(pieces):
        source = weights_ref.at[:, pl.ds(pl.multiple_of(columns + start, 128), stop - start)]
        target = target_ref.at[:, start - first : stop - first]
        copies.append((start, stop, pltpu.make_async_copy(source, target, sems.at[i])))
        copies[-1][2].start()
    return copies


def part_of(rows_ref, held_ref, start, stop):
    return jnp.dot(rows_ref[...], held_ref[:, start:stop], preferred_element_type=f32)


def mixing_kernel(outer_ref, query_ref, held_ref, up_ref, rows_ref):
    rows_ref[...] = (query_ref[...] * outer_ref[...].T.astype(f32)).astype(bf16)
    for start, stop in LEFT:
        up_ref[:, start:stop] = part_of(rows_ref, held_ref, start, stop).astype(bf16)


def far_kernel(rows_ref, rest_ref, down_ref):
    for start, stop in RIGHT:
        down_ref[:, start - UP : stop - UP] = part_of(rows_ref, rest_ref, start - UP, stop - UP).astype(bf16)


def near_kernel(rows_ref, near_ref, up_ref, down_ref):
    for start, stop in RIGHT:
        up_ref[:, start - UP : stop - UP] = part_of(rows_ref, near_ref, start, stop).astype(bf16)
    for start, stop in LEFT:
        down_ref[:, start:stop] = part_of(rows_ref, near_ref, start, stop).astype(bf16)


def adding_kernel(rows_ref, later_ref, far_up_ref, far_down_ref, up_ref, down_ref):
    for start, stop in LEFT:
        total = part_of(rows_ref, later_ref, start, stop)
        up_ref[:, start:stop] = (total + far_up_ref[:, start:stop].astype(f32)).astype(bf16)
    for start, stop in RIGHT:
        here = slice(start - UP, stop - UP)
        total = part_of(rows_ref, later_ref, start, stop)
        down_ref[:, here] = (total + far_down_ref[:, here].astype(f32)).astype(bf16)


def own_kernel(rows_ref, near_up_ref, near_down_ref, weights_ref, out_ref, held_ref, sems):
    for start, stop, copy in fetch(weights_ref, held_ref, sems, 0, LEFT + RIGHT):
        copy.wait()
        arrived = near_down_ref[:, start:stop] if start < UP else near_up_ref[:, start - UP : stop - UP]
        out_ref[:, start:stop] = part_of(rows_ref, held_ref, start, stop) + arrived.astype(f32)


def last_kernel(own_ref, both_up_ref, both_down_ref, out_ref):
    for part, arrived_ref in ((slice(0, UP), both_up_ref), (slice(UP, WIDE), both_down_ref)):
        out_ref[:, part] = (own_ref[:, part] + arrived_ref[...].astype(f32)).astype(bf16)


TABLES = 4
RING = 4
WIDE = 2048
UP = 1152
LEFT = ((0, 640), (640, UP))
RIGHT = ((UP, 1664), (1664, WIDE))
SENT = 3
EDGE = 16
VMEM = pl.BlockSpec(memory_space=pltpu.VMEM)
HBM = pl.BlockSpec(memory_space=pltpu.HBM)


def share(kernel, arrays, outs, held):
    return pl.pallas_call(
        kernel,
        in_specs=[VMEM] * (len(arrays) - 1) + [HBM],
        out_specs=[VMEM] * len(outs),
        out_shape=[pltpu.VMEM(shape, dtype) for shape, dtype in outs],
        scratch_shapes=[
            pltpu.VMEM((arrays[-1].shape[0], held), bf16),
            pltpu.SemaphoreType.DMA((2 * len(LEFT) + len(RIGHT),)),
        ],
        cost_estimate=pl.CostEstimate(flops=2**31, bytes_accessed=2**21, transcendentals=0),
        compiler_params=pltpu.CompilerParams(vmem_limit_bytes=16 * 2**20),
    )(*arrays)


def plain(kernel, arrays, outs):
    return pl.pallas_call(
        kernel,
        in_specs=[VMEM] * len(arrays),
        out_specs=[VMEM] * len(outs),
        out_shape=[pltpu.VMEM(shape, dtype) for shape, dtype in outs],
        cost_estimate=pl.CostEstimate(flops=2**31, bytes_accessed=2**21, transcendentals=0),
        compiler_params=pltpu.CompilerParams(vmem_limit_bytes=8 * 2**20),
    )(*arrays)


def project(outer, query, weights, held, rest, near, later):
    up = [(i, (i + 1) % RING) for i in range(RING)]
    down = [(i, (i - 1) % RING) for i in range(RING)]
    left, right = ((ROWS, UP), bf16), ((ROWS, WIDE - UP), bf16)
    far_up, rows = plain(mixing_kernel, (outer, query, held), [left, (query.shape, bf16)])
    far_up = lax.ppermute(far_up, "ch", up)
    (far_down,) = plain(far_kernel, (rows, rest), [right])
    far_down = lax.ppermute(far_down, "ch", down)
    near_up, near_down = plain(near_kernel, (rows, near), [right, left])
    near_up = lax.ppermute(near_up, "ch", up)
    near_down = lax.ppermute(near_down, "ch", down)
    both_up, both_down = plain(adding_kernel, (rows, later, far_up, far_down), [left, right])
    both_up = lax.ppermute(both_up, "ch", up)
    both_down = lax.ppermute(both_down, "ch", down)
    (own,) = share(own_kernel, (rows, near_up, near_down, weights), [((ROWS, WIDE), f32)], WIDE)
    return pl.pallas_call(
        last_kernel,
        in_specs=[VMEM] * 3,
        out_specs=VMEM,
        out_shape=jax.ShapeDtypeStruct((ROWS, WIDE), bf16),
        compiler_params=pltpu.CompilerParams(vmem_limit_bytes=16 * 2**20),
    )(own, both_up, both_down)


def stage(after, weights, *arrays):
    arrays = [pltpu.with_memory_space_constraint(array, pltpu.HBM) for array in arrays]
    parts = [pltpu.HBM((weights.shape[0], wide), bf16) for wide in (WIDE - UP, WIDE, WIDE)]
    return pl.pallas_call(
        stage_kernel,
        in_specs=[pl.BlockSpec(memory_space=pl.ANY)] + [HBM] * (len(arrays) + 1),
        out_specs=[VMEM] * len(arrays) + [HBM] * len(parts),
        out_shape=[pltpu.VMEM(array.shape, array.dtype) for array in arrays] + parts,
        scratch_shapes=[
            pltpu.VMEM((weights.shape[0], 3 * WIDE - UP), bf16),
            pltpu.SemaphoreType.DMA((len(arrays) + 2 * len(LEFT) + 3 * len(RIGHT),)),
        ],
        compiler_params=pltpu.CompilerParams(vmem_limit_bytes=16 * 2**20),
    )(after, *arrays, weights)


def convolve(*arrays):
    channels = arrays[-1].shape[0]
    return pl.pallas_call(
        conv_kernel,
        in_specs=[VMEM] * 6 + [HBM],
        out_specs=[VMEM, VMEM],
        out_shape=[
            pltpu.VMEM((PARTS, GROUP, ROWS), bf16),
            pltpu.VMEM((channels, UP), bf16),
        ],
        scratch_shapes=[
            pltpu.VMEM((PARTS, GROUP, ROWS), f32),
            pltpu.VMEM((4, 8, 2, SLAB, ROWS), f32),
            pltpu.VMEM((2, 2, PARTS * GROUP, 2 * ROWS), bf16),
            pltpu.VMEM((PARTS * GROUP, 2 * ROWS), f32),
            pltpu.SemaphoreType.DMA((len(LEFT),)),
        ],
        compiler_params=pltpu.CompilerParams(vmem_limit_bytes=16 * 2**20),
    )(*arrays)


def on_device(streams, short_taps, long_filter, skip_gain, out_weights):
    channels = streams.shape[2]
    streams = pltpu.with_memory_space_constraint(streams, pltpu.HBM)
    weights = pltpu.with_memory_space_constraint(out_weights, pltpu.HBM)
    packed, edge = pl.pallas_call(
        exchange_kernel,
        in_specs=[HBM, HBM],
        out_specs=[VMEM, VMEM],
        out_shape=[
            pltpu.VMEM((PARTS, SENT * GROUP, ROWS), bf16),
            pltpu.VMEM((EDGE, channels), bf16),
        ],
        scratch_shapes=[
            pltpu.VMEM((SENT - 1, ROWS, channels), bf16),
            pltpu.VMEM((ROWS, channels), f32),
            pltpu.SemaphoreType.DMA((SENT + 1,)),
        ],
        compiler_params=pltpu.CompilerParams(vmem_limit_bytes=8 * 2**20),
    )(streams, pltpu.with_memory_space_constraint(long_filter, pltpu.HBM))
    high, low, twists = (jnp.asarray(table) for table in tables())
    high, low, twists, short_taps, *parts = stage(edge, weights, high, low, twists, short_taps)
    arrived = lax.all_to_all(packed, "seq", 0, 0, tiled=True)
    edge = lax.ppermute(edge, "seq", [(i, i + 1) for i in range(PARTS - 1)])
    first = lax.axis_index("seq") * GROUP
    taps = lax.dynamic_slice_in_dim(short_taps[1:].reshape((SENT - 1) * SHORT, channels), first, GROUP, 1)
    taps = jnp.broadcast_to(taps[:, :, None], ((SENT - 1) * SHORT, GROUP, ROWS))
    skip = jnp.broadcast_to(lax.dynamic_slice_in_dim(skip_gain, first, GROUP, 0)[:, None], (GROUP, ROWS))
    outer, held = convolve(arrived, taps, skip, high, low, twists, weights)
    query = pl.pallas_call(
        query_kernel,
        in_specs=[HBM, VMEM, VMEM, VMEM],
        out_specs=VMEM,
        out_shape=pltpu.VMEM((ROWS, channels), f32),
        scratch_shapes=[pltpu.VMEM((ROWS, channels), bf16), pltpu.SemaphoreType.DMA((1,))],
        compiler_params=pltpu.CompilerParams(vmem_limit_bytes=8 * 2**20),
    )(streams, edge, short_taps, held)
    outer = lax.all_to_all(outer, "seq", 0, 0, tiled=True)
    return project(outer.reshape(channels, ROWS), query, weights, held, *parts)


def solution(mesh):
    return jax.shard_map(
        on_device,
        mesh=mesh,
        in_specs=(
            P(None, "seq", "ch"),
            P(None, None, "ch"),
            P("seq", "ch"),
            P("ch"),
            P("ch", None),
        ),
        out_specs=P("seq", "ch"),
        check_vma=False,
    )
```

```python
import functools
import math

import jax
import jax.numpy as jnp
import numpy as np
from jax import lax
from jax.experimental import pallas as pl
from jax.experimental.pallas import tpu as pltpu
from jax.sharding import PartitionSpec as P

SHORT = 3
ROWS = 128
PARTS = 32
GROUP = 32
SLAB = 16
POINTS = PARTS * ROWS
f32 = jnp.float32
bf16 = jnp.bfloat16


def tables():
    r = np.arange(ROWS)
    angle = 2.0 * np.pi * (np.outer(r, r) % ROWS) / ROWS
    cosine, sine = np.cos(angle), np.sin(angle)
    matrix = np.block([[cosine, -sine], [sine, cosine]])
    high = matrix.astype(np.float32).astype(bf16)
    low = (matrix - high.astype(np.float64)).astype(np.float32).astype(bf16)
    j = np.arange(PARTS)
    twist = 2.0 * np.pi * np.outer(4 * j + 1, r) / (4 * POINTS)
    twists = np.stack([np.cos(twist), np.sin(twist)], axis=1).astype(np.float32)
    return high, low, twists


def turned(value, turns):
    real, imag = value
    eighth = turns * 8 % 8
    if eighth == 0:
        return real, imag
    if eighth == 2:
        return -imag, real
    if eighth == 4:
        return -real, -imag
    if eighth == 6:
        return imag, -real
    if eighth in (1, 3, 5, 7):
        half = math.sqrt(0.5)
        total, apart = (real + imag) * half, (real - imag) * half
        return {1: (apart, total), 3: (-total, apart), 5: (-apart, -total), 7: (total, -apart)}[int(eighth)]
    c, s = math.cos(2.0 * math.pi * turns), math.sin(2.0 * math.pi * turns)
    return real * c - imag * s, real * s + imag * c


def plus(a, b):
    return a[0] + b[0], a[1] + b[1]


def minus(a, b):
    return a[0] - b[0], a[1] - b[1]


def small_transform(values, sign):
    count = len(values)
    if count == 1:
        return values
    even = small_transform(values[0::2], sign)
    odd = small_transform(values[1::2], sign)
    odd = [turned(value, sign * k / count) for k, value in enumerate(odd)]
    return [plus(a, b) for a, b in zip(even, odd)] + [minus(a, b) for a, b in zip(even, odd)]


def exchange_kernel(streams_ref, filter_ref, out_ref, edge_ref, rows_ref, taps_ref, packed_ref, sems, out_sems):
    copies = [pltpu.make_async_copy(streams_ref.at[i + 1], rows_ref.at[i], sems.at[i]) for i in range(SENT - 1)]
    copies.append(pltpu.make_async_copy(filter_ref, taps_ref, sems.at[SENT - 1]))
    edge = pltpu.make_async_copy(streams_ref.at[0, ROWS - EDGE :], edge_ref, sems.at[SENT])
    for copy in copies:
        copy.start()
    edge.start()
    wide = 8 * GROUP
    leaving = []
    for j, copy in enumerate(copies):
        copy.wait()
        for first in range(0, PARTS * GROUP, wide):
            here = slice(first, first + wide)
            block = rows_ref[j, :, here] if j < SENT - 1 else taps_ref[:, here].astype(bf16)
            parts = pl.ds(first // GROUP, wide // GROUP)
            packed_ref[parts, j * GROUP : (j + 1) * GROUP, :] = block.T.reshape(wide // GROUP, GROUP, ROWS)
        own = (slice(None), slice(j * GROUP, (j + 1) * GROUP))
        leaving.append(pltpu.make_async_copy(packed_ref.at[own], out_ref.at[own], out_sems.at[j]))
        leaving[-1].start()
    edge.wait()
    for copy in leaving:
        copy.wait()


def stage_kernel(*refs):
    sems, bounce_ref = refs[-1], refs[-2]
    tables_in, weights_ref = refs[1 : 1 + TABLES], refs[1 + TABLES]
    tables_out = refs[2 + TABLES : 2 + 2 * TABLES]
    rest_ref, near_ref, later_ref = refs[-5:-2]
    copies = [
        pltpu.make_async_copy(source, target, sems.at[i]) for i, (source, target) in enumerate(zip(tables_in, tables_out))
    ]
    for copy in copies:
        copy.start()
    count, arriving = TABLES, []
    for target_ref, at, away, pieces, first in (
        (near_ref, 0, 1, RIGHT, 0), (near_ref, 0, RING - 1, LEFT, 0), (rest_ref, WIDE, 2, RIGHT, UP),
        (later_ref, 2 * WIDE - UP, 1, LEFT, 0), (later_ref, 2 * WIDE - UP, RING - 1, RIGHT, 0),
    ):
        held_ref = bounce_ref.at[:, at : at + target_ref.shape[1]]
        for start, stop, copy in fetch(weights_ref, held_ref, sems.at[count:], away, pieces, first):
            here = slice(start - first, stop - first)
            arriving.append((copy, pltpu.make_async_copy(held_ref.at[:, here], target_ref.at[:, here], sems.at[count])))
            count += 1
    for copy, onward in arriving:
        copy.wait()
        onward.start()
        copies.append(onward)
    for copy in copies:
        copy.wait()


def query_kernel(streams_ref, edge_ref, taps_ref, held_ref, out_ref, rows_ref, sem):
    copy = pltpu.make_async_copy(streams_ref.at[0], rows_ref, sem.at[0])
    copy.start()
    copy.wait()
    now = rows_ref[...].astype(f32)
    earlier = edge_ref[...].astype(f32)
    row = lax.broadcasted_iota(jnp.int32, now.shape, 0)
    last, before_last = earlier[EDGE - 1 :, :], earlier[EDGE - 2 : EDGE - 1, :]
    one = jnp.where(row == 0, last, pltpu.roll(now, 1, 0))
    two = jnp.where(row == 0, before_last, jnp.where(row == 1, last, pltpu.roll(now, 2, 0)))
    out_ref[...] = taps_ref[0, 0:1, :] * now + taps_ref[0, 1:2, :] * one + taps_ref[0, 2:3, :] * two


def split(value):
    high = value.astype(bf16)
    return high, (value - high.astype(f32)).astype(bf16)


def conv_kernel(
    x_ref, taps_ref, skip_ref, high_ref, low_ref, twists_ref, weights_ref,
    out_ref, held_ref, gated_ref, first_ref, left_ref, back_ref, sems,
):
    copies = fetch(weights_ref, held_ref, sems, 2, LEFT)
    lane = lax.broadcasted_iota(jnp.int32, (SLAB, ROWS), 1)

    def rows_of(j, offset):
        return pl.ds(pl.multiple_of(j * GROUP + offset, SLAB), SLAB)

    def short(stream, offset):
        taps = [taps_ref[stream * SHORT + i, pl.ds(offset, SLAB), :] for i in range(SHORT)]
        before = [jnp.zeros((SLAB, ROWS), f32)] * 2
        for s in range(PARTS):
            now = x_ref[s, rows_of(stream, offset), :].astype(f32)
            moved = [pltpu.roll(now, i, 1) for i in (1, 2)]
            total = taps[0] * now
            for i in (1, 2):
                total = total + taps[i] * jnp.where(lane < i, before[i - 1], moved[i - 1])
            before = moved
            yield total

    def forward(slot, offset, load):
        for a in range(8):
            values = []
            for q in range(4):
                value = load(a + 8 * q)
                angle = -2.0 * math.pi * q / 16
                values.append((value * math.cos(angle), value * math.sin(angle)) if q else (value, jnp.zeros_like(value)))
            for m, value in enumerate(small_transform(values, -1)):
                real, imag = turned(value, -a * (4 * m + 1) / 128)
                first_ref[m, a, 0] = real
                first_ref[m, a, 1] = imag
        for m in range(4):
            values = [(first_ref[m, a, 0], first_ref[m, a, 1]) for a in range(8)]
            for p, (real, imag) in enumerate(small_transform(values, -1)):
                j = 4 * p + m
                c, s = twists_ref[j, 0][None, :], twists_ref[j, 1][None, :]
                for half, part in enumerate((real * c + imag * s, imag * c - real * s)):
                    high, low = split(part)
                    left_ref[slot, 0, rows_of(j, offset), half * ROWS : (half + 1) * ROWS] = high
                    left_ref[slot, 1, rows_of(j, offset), half * ROWS : (half + 1) * ROWS] = low

    @pl.loop(0, GROUP // SLAB)
    def _(step):
        offset = pl.multiple_of(step * SLAB, SLAB)
        for s, (key, value) in enumerate(zip(short(0, offset), short(1, offset))):
            gated_ref[s, pl.ds(offset, SLAB), :] = key * value
        forward(0, offset, lambda s: gated_ref[s, pl.ds(offset, SLAB), :])
        forward(1, offset, lambda s: x_ref[s, rows_of(SENT - 1, offset), :].astype(f32))

    matrix = jnp.concatenate([high_ref[...], low_ref[...], high_ref[...]], axis=0)

    def product(high, low):
        return jnp.dot(jnp.concatenate([low, high, high], axis=1), matrix, preferred_element_type=f32)

    block = 256
    blocks = [pl.ds(start, block) for start in range(0, PARTS * GROUP, block)]
    for rows in blocks:
        signal = product(left_ref[0, 0, rows, :], left_ref[0, 1, rows, :])
        taps = product(left_ref[1, 0, rows, :], left_ref[1, 1, rows, :])
        a, b = signal[:, :ROWS], signal[:, ROWS:]
        c, d = taps[:, :ROWS], taps[:, ROWS:]
        real, imag = split((a * c - b * d) * (1.0 / POINTS)), split((a * d + b * c) * (-1.0 / POINTS))
        left_ref[0, 0, rows, :] = jnp.concatenate([real[0], imag[0]], axis=1)
        left_ref[0, 1, rows, :] = jnp.concatenate([real[1], imag[1]], axis=1)
    for rows in blocks:
        back_ref[rows, :] = product(left_ref[0, 0, rows, :], left_ref[0, 1, rows, :])

    @pl.loop(0, GROUP // SLAB)
    def _(step):
        offset = pl.multiple_of(step * SLAB, SLAB)
        for m in range(4):
            values = []
            for p in range(8):
                j = 4 * p + m
                real = back_ref[rows_of(j, offset), :ROWS]
                imag = -back_ref[rows_of(j, offset), ROWS:]
                c, s = twists_ref[j, 0][None, :], twists_ref[j, 1][None, :]
                values.append((real * c - imag * s, real * s + imag * c))
            for a, value in enumerate(small_transform(values, 1)):
                real, imag = turned(value, a * (4 * m + 1) / 128)
                first_ref[m, a, 0] = real
                first_ref[m, a, 1] = imag
        skip = skip_ref[pl.ds(offset, SLAB), :]
        for a in range(8):
            values = [(first_ref[m, a, 0], first_ref[m, a, 1]) for m in range(4)]
            for q, (real, imag) in enumerate(small_transform(values, 1)):
                angle = 2.0 * math.pi * q / 16
                conv = real * math.cos(angle) - imag * math.sin(angle) if q else real
                s = a + 8 * q
                gated = gated_ref[s, pl.ds(offset, SLAB), :]
                out_ref[s, pl.ds(offset, SLAB), :] = (conv + skip * gated).astype(bf16)

    for _, _, copy in copies:
        copy.wait()


def fetch(weights_ref, target_ref, sems, away, pieces, first=0):
    columns = (lax.axis_index("ch") + away) % RING * WIDE
    copies = []
    for i, (start, stop) in enumerate(pieces):
        source = weights_ref.at[:, pl.ds(pl.multiple_of(columns + start, 128), stop - start)]
        target = target_ref.at[:, start - first : stop - first]
        copies.append((start, stop, pltpu.make_async_copy(source, target, sems.at[i])))
        copies[-1][2].start()
    return copies


def part_of(rows_ref, held_ref, start, stop):
    return jnp.dot(rows_ref[...], held_ref[:, start:stop], preferred_element_type=f32)


def mixing_kernel(outer_ref, query_ref, held_ref, up_ref, rows_ref):
    rows_ref[...] = (query_ref[...] * outer_ref[...].T.astype(f32)).astype(bf16)
    for start, stop in LEFT:
        up_ref[:, start:stop] = part_of(rows_ref, held_ref, start, stop).astype(bf16)


def far_kernel(rows_ref, rest_ref, down_ref):
    for start, stop in RIGHT:
        down_ref[:, start - UP : stop - UP] = part_of(rows_ref, rest_ref, start - UP, stop - UP).astype(bf16)


def near_kernel(rows_ref, near_ref, up_ref, down_ref):
    for start, stop in RIGHT:
        up_ref[:, start - UP : stop - UP] = part_of(rows_ref, near_ref, start, stop).astype(bf16)
    for start, stop in LEFT:
        down_ref[:, start:stop] = part_of(rows_ref, near_ref, start, stop).astype(bf16)


def adding_kernel(rows_ref, later_ref, far_up_ref, far_down_ref, up_ref, down_ref):
    for start, stop in LEFT:
        total = part_of(rows_ref, later_ref, start, stop)
        up_ref[:, start:stop] = (total + far_up_ref[:, start:stop].astype(f32)).astype(bf16)
    for start, stop in RIGHT:
        here = slice(start - UP, stop - UP)
        total = part_of(rows_ref, later_ref, start, stop)
        down_ref[:, here] = (total + far_down_ref[:, here].astype(f32)).astype(bf16)


def own_kernel(rows_ref, near_up_ref, near_down_ref, weights_ref, out_ref, held_ref, sems):
    for start, stop, copy in fetch(weights_ref, held_ref, sems, 0, LEFT + RIGHT):
        copy.wait()
        arrived = near_down_ref[:, start:stop] if start < UP else near_up_ref[:, start - UP : stop - UP]
        out_ref[:, start:stop] = part_of(rows_ref, held_ref, start, stop) + arrived.astype(f32)


def last_kernel(own_ref, both_up_ref, both_down_ref, out_ref, rows_ref, sems):
    copies = []
    for start in range(0, ROWS, LAST):
        here = slice(start, start + LAST)
        for part, arrived_ref in ((slice(0, UP), both_up_ref), (slice(UP, WIDE), both_down_ref)):
            rows_ref[here, part] = (own_ref[here, part] + arrived_ref[here, :].astype(f32)).astype(bf16)
        copies.append(pltpu.make_async_copy(rows_ref.at[here], out_ref.at[here], sems.at[start // LAST]))
        copies[-1].start()
    for copy in copies:
        copy.wait()


LAST = 32
TABLES = 4
RING = 4
WIDE = 2048
UP = 1152
LEFT = ((0, 640), (640, UP))
RIGHT = ((UP, 1664), (1664, WIDE))
SENT = 3
EDGE = 16
VMEM = pl.BlockSpec(memory_space=pltpu.VMEM)
HBM = pl.BlockSpec(memory_space=pltpu.HBM)


def share(kernel, arrays, outs, held):
    return pl.pallas_call(
        kernel,
        in_specs=[VMEM] * (len(arrays) - 1) + [HBM],
        out_specs=[VMEM] * len(outs),
        out_shape=[pltpu.VMEM(shape, dtype) for shape, dtype in outs],
        scratch_shapes=[
            pltpu.VMEM((arrays[-1].shape[0], held), bf16),
            pltpu.SemaphoreType.DMA((2 * len(LEFT) + len(RIGHT),)),
        ],
        cost_estimate=pl.CostEstimate(flops=2**31, bytes_accessed=2**21, transcendentals=0),
        compiler_params=pltpu.CompilerParams(vmem_limit_bytes=16 * 2**20),
    )(*arrays)


def plain(kernel, arrays, outs):
    return pl.pallas_call(
        kernel,
        in_specs=[VMEM] * len(arrays),
        out_specs=[VMEM] * len(outs),
        out_shape=[pltpu.VMEM(shape, dtype) for shape, dtype in outs],
        cost_estimate=pl.CostEstimate(flops=2**31, bytes_accessed=2**21, transcendentals=0),
        compiler_params=pltpu.CompilerParams(vmem_limit_bytes=8 * 2**20),
    )(*arrays)


def project(outer, query, weights, held, rest, near, later):
    up = [(i, (i + 1) % RING) for i in range(RING)]
    down = [(i, (i - 1) % RING) for i in range(RING)]
    left, right = ((ROWS, UP), bf16), ((ROWS, WIDE - UP), bf16)
    far_up, rows = plain(mixing_kernel, (outer, query, held), [left, (query.shape, bf16)])
    far_up = lax.ppermute(far_up, "ch", up)
    (far_down,) = plain(far_kernel, (rows, rest), [right])
    far_down = lax.ppermute(far_down, "ch", down)
    near_up, near_down = plain(near_kernel, (rows, near), [right, left])
    near_up = lax.ppermute(near_up, "ch", up)
    near_down = lax.ppermute(near_down, "ch", down)
    both_up, both_down = plain(adding_kernel, (rows, later, far_up, far_down), [left, right])
    both_up = lax.ppermute(both_up, "ch", up)
    both_down = lax.ppermute(both_down, "ch", down)
    (own,) = share(own_kernel, (rows, near_up, near_down, weights), [((ROWS, WIDE), f32)], WIDE)
    return pl.pallas_call(
        last_kernel,
        in_specs=[VMEM] * 3,
        out_specs=HBM,
        out_shape=jax.ShapeDtypeStruct((ROWS, WIDE), bf16),
        scratch_shapes=[pltpu.VMEM((ROWS, WIDE), bf16), pltpu.SemaphoreType.DMA((ROWS // LAST,))],
        compiler_params=pltpu.CompilerParams(vmem_limit_bytes=16 * 2**20),
    )(own, both_up, both_down)


def stage(after, weights, *arrays):
    arrays = [pltpu.with_memory_space_constraint(array, pltpu.HBM) for array in arrays]
    parts = [pltpu.HBM((weights.shape[0], wide), bf16) for wide in (WIDE - UP, WIDE, WIDE)]
    return pl.pallas_call(
        stage_kernel,
        in_specs=[pl.BlockSpec(memory_space=pl.ANY)] + [HBM] * (len(arrays) + 1),
        out_specs=[VMEM] * len(arrays) + [HBM] * len(parts),
        out_shape=[pltpu.VMEM(array.shape, array.dtype) for array in arrays] + parts,
        scratch_shapes=[
            pltpu.VMEM((weights.shape[0], 3 * WIDE - UP), bf16),
            pltpu.SemaphoreType.DMA((len(arrays) + 2 * len(LEFT) + 3 * len(RIGHT),)),
        ],
        compiler_params=pltpu.CompilerParams(vmem_limit_bytes=16 * 2**20),
    )(after, *arrays, weights)


def convolve(*arrays):
    channels = arrays[-1].shape[0]
    return pl.pallas_call(
        conv_kernel,
        in_specs=[VMEM] * 6 + [HBM],
        out_specs=[VMEM, VMEM],
        out_shape=[
            pltpu.VMEM((PARTS, GROUP, ROWS), bf16),
            pltpu.VMEM((channels, UP), bf16),
        ],
        scratch_shapes=[
            pltpu.VMEM((PARTS, GROUP, ROWS), f32),
            pltpu.VMEM((4, 8, 2, SLAB, ROWS), f32),
            pltpu.VMEM((2, 2, PARTS * GROUP, 2 * ROWS), bf16),
            pltpu.VMEM((PARTS * GROUP, 2 * ROWS), f32),
            pltpu.SemaphoreType.DMA((len(LEFT),)),
        ],
        compiler_params=pltpu.CompilerParams(vmem_limit_bytes=16 * 2**20),
    )(*arrays)


def on_device(streams, short_taps, long_filter, skip_gain, out_weights):
    channels = streams.shape[2]
    streams = pltpu.with_memory_space_constraint(streams, pltpu.HBM)
    weights = pltpu.with_memory_space_constraint(out_weights, pltpu.HBM)
    packed, edge = pl.pallas_call(
        exchange_kernel,
        in_specs=[HBM, HBM],
        out_specs=[HBM, VMEM],
        out_shape=[
            pltpu.HBM((PARTS, SENT * GROUP, ROWS), bf16),
            pltpu.VMEM((EDGE, channels), bf16),
        ],
        scratch_shapes=[
            pltpu.VMEM((SENT - 1, ROWS, channels), bf16),
            pltpu.VMEM((ROWS, channels), f32),
            pltpu.VMEM((PARTS, SENT * GROUP, ROWS), bf16),
            pltpu.SemaphoreType.DMA((SENT + 1,)),
            pltpu.SemaphoreType.DMA((SENT,)),
        ],
        compiler_params=pltpu.CompilerParams(vmem_limit_bytes=8 * 2**20),
    )(streams, pltpu.with_memory_space_constraint(long_filter, pltpu.HBM))
    high, low, twists = (jnp.asarray(table) for table in tables())
    high, low, twists, short_taps, *parts = stage(edge, weights, high, low, twists, short_taps)
    arrived = lax.all_to_all(packed, "seq", 0, 0, tiled=True)
    edge = lax.ppermute(edge, "seq", [(i, i + 1) for i in range(PARTS - 1)])
    first = lax.axis_index("seq") * GROUP
    taps = lax.dynamic_slice_in_dim(short_taps[1:].reshape((SENT - 1) * SHORT, channels), first, GROUP, 1)
    taps = jnp.broadcast_to(taps[:, :, None], ((SENT - 1) * SHORT, GROUP, ROWS))
    skip = jnp.broadcast_to(lax.dynamic_slice_in_dim(skip_gain, first, GROUP, 0)[:, None], (GROUP, ROWS))
    outer, held = convolve(arrived, taps, skip, high, low, twists, weights)
    query = pl.pallas_call(
        query_kernel,
        in_specs=[HBM, VMEM, VMEM, VMEM],
        out_specs=VMEM,
        out_shape=pltpu.VMEM((ROWS, channels), f32),
        scratch_shapes=[pltpu.VMEM((ROWS, channels), bf16), pltpu.SemaphoreType.DMA((1,))],
        compiler_params=pltpu.CompilerParams(vmem_limit_bytes=8 * 2**20),
    )(streams, edge, short_taps, held)
    outer = lax.all_to_all(outer, "seq", 0, 0, tiled=True)
    return project(outer.reshape(channels, ROWS), query, weights, held, *parts)


def solution(mesh):
    return jax.shard_map(
        on_device,
        mesh=mesh,
        in_specs=(
            P(None, "seq", "ch"),
            P(None, None, "ch"),
            P("seq", "ch"),
            P("ch"),
            P("ch", None),
        ),
        out_specs=P("seq", "ch"),
        check_vma=False,
    )
```

```python
import functools
import math

import jax
import jax.numpy as jnp
import numpy as np
from jax import lax
from jax.experimental import pallas as pl
from jax.experimental.pallas import tpu as pltpu
from jax.sharding import PartitionSpec as P

SHORT = 3
ROWS = 128
PARTS = 32
GROUP = 32
SLAB = 16
POINTS = PARTS * ROWS
f32 = jnp.float32
bf16 = jnp.bfloat16


def tables():
    r = np.arange(ROWS)
    angle = 2.0 * np.pi * (np.outer(r, r) % ROWS) / ROWS
    cosine, sine = np.cos(angle), np.sin(angle)
    matrix = np.block([[cosine, -sine], [sine, cosine]])
    high = matrix.astype(np.float32).astype(bf16)
    low = (matrix - high.astype(np.float64)).astype(np.float32).astype(bf16)
    j = np.arange(PARTS)
    twist = 2.0 * np.pi * np.outer(4 * j + 1, r) / (4 * POINTS)
    twists = np.stack([np.cos(twist), np.sin(twist)], axis=1).astype(np.float32)
    return high, low, twists


def turned(value, turns):
    real, imag = value
    eighth = turns * 8 % 8
    if eighth == 0:
        return real, imag
    if eighth == 2:
        return -imag, real
    if eighth == 4:
        return -real, -imag
    if eighth == 6:
        return imag, -real
    if eighth in (1, 3, 5, 7):
        half = math.sqrt(0.5)
        total, apart = (real + imag) * half, (real - imag) * half
        return {1: (apart, total), 3: (-total, apart), 5: (-apart, -total), 7: (total, -apart)}[int(eighth)]
    c, s = math.cos(2.0 * math.pi * turns), math.sin(2.0 * math.pi * turns)
    return real * c - imag * s, real * s + imag * c


def plus(a, b):
    return a[0] + b[0], a[1] + b[1]


def minus(a, b):
    return a[0] - b[0], a[1] - b[1]


def small_transform(values, sign):
    count = len(values)
    if count == 1:
        return values
    even = small_transform(values[0::2], sign)
    odd = small_transform(values[1::2], sign)
    odd = [turned(value, sign * k / count) for k, value in enumerate(odd)]
    return [plus(a, b) for a, b in zip(even, odd)] + [minus(a, b) for a, b in zip(even, odd)]


def exchange_kernel(streams_ref, filter_ref, out_ref, edge_ref, rows_ref, taps_ref, packed_ref, sems, out_sems):
    copies = [pltpu.make_async_copy(streams_ref.at[i + 1], rows_ref.at[i], sems.at[i]) for i in range(SENT - 1)]
    copies.append(pltpu.make_async_copy(filter_ref, taps_ref, sems.at[SENT - 1]))
    edge = pltpu.make_async_copy(streams_ref.at[0, ROWS - EDGE :], edge_ref, sems.at[SENT])
    for copy in copies:
        copy.start()
    edge.start()
    wide = 8 * GROUP
    leaving = []
    for j, copy in enumerate(copies):
        copy.wait()
        for first in range(0, PARTS * GROUP, wide):
            here = slice(first, first + wide)
            block = rows_ref[j, :, here] if j < SENT - 1 else taps_ref[:, here].astype(bf16)
            parts = pl.ds(first // GROUP, wide // GROUP)
            packed_ref[parts, j * GROUP : (j + 1) * GROUP, :] = block.T.reshape(wide // GROUP, GROUP, ROWS)
        own = (slice(None), slice(j * GROUP, (j + 1) * GROUP))
        leaving.append(pltpu.make_async_copy(packed_ref.at[own], out_ref.at[own], out_sems.at[j]))
        leaving[-1].start()
    edge.wait()
    for copy in leaving:
        copy.wait()


def stage_kernel(*refs):
    sems, bounce_ref = refs[-1], refs[-2]
    tables_in, weights_ref = refs[1 : 1 + TABLES], refs[1 + TABLES]
    tables_out = refs[2 + TABLES : 2 + 2 * TABLES]
    rest_ref, near_ref, later_ref = refs[-5:-2]
    copies = [
        pltpu.make_async_copy(source, target, sems.at[i]) for i, (source, target) in enumerate(zip(tables_in, tables_out))
    ]
    for copy in copies:
        copy.start()
    count, arriving = TABLES, []
    for target_ref, at, away, pieces, first in (
        (near_ref, 0, 1, RIGHT, 0), (near_ref, 0, RING - 1, LEFT, 0), (rest_ref, WIDE, 2, RIGHT, UP),
        (later_ref, 2 * WIDE - UP, 1, LEFT, 0), (later_ref, 2 * WIDE - UP, RING - 1, RIGHT, 0),
    ):
        held_ref = bounce_ref.at[:, at : at + target_ref.shape[1]]
        for start, stop, copy in fetch(weights_ref, held_ref, sems.at[count:], away, pieces, first):
            here = slice(start - first, stop - first)
            arriving.append((copy, pltpu.make_async_copy(held_ref.at[:, here], target_ref.at[:, here], sems.at[count])))
            count += 1
    for copy, onward in arriving:
        copy.wait()
        onward.start()
        copies.append(onward)
    for copy in copies:
        copy.wait()


def query_kernel(streams_ref, edge_ref, taps_ref, held_ref, out_ref, rows_ref, sem):
    copy = pltpu.make_async_copy(streams_ref.at[0], rows_ref, sem.at[0])
    copy.start()
    copy.wait()
    now = rows_ref[...].astype(f32)
    earlier = edge_ref[...].astype(f32)
    row = lax.broadcasted_iota(jnp.int32, now.shape, 0)
    last, before_last = earlier[EDGE - 1 :, :], earlier[EDGE - 2 : EDGE - 1, :]
    one = jnp.where(row == 0, last, pltpu.roll(now, 1, 0))
    two = jnp.where(row == 0, before_last, jnp.where(row == 1, last, pltpu.roll(now, 2, 0)))
    out_ref[...] = taps_ref[0, 0:1, :] * now + taps_ref[0, 1:2, :] * one + taps_ref[0, 2:3, :] * two


def split(value):
    high = value.astype(bf16)
    return high, (value - high.astype(f32)).astype(bf16)


def conv_kernel(
    x_ref, taps_ref, skip_ref, high_ref, low_ref, twists_ref, weights_ref,
    out_ref, held_ref, gated_ref, first_ref, left_ref, back_ref, sems,
):
    copies = fetch(weights_ref, held_ref, sems, 2, LEFT)
    lane = lax.broadcasted_iota(jnp.int32, (SLAB, ROWS), 1)

    def rows_of(j, offset):
        return pl.ds(pl.multiple_of(j * GROUP + offset, SLAB), SLAB)

    def short(stream, offset):
        taps = [taps_ref[stream * SHORT + i, pl.ds(offset, SLAB), :] for i in range(SHORT)]
        before = [jnp.zeros((SLAB, ROWS), f32)] * 2
        for s in range(PARTS):
            now = x_ref[s, rows_of(stream, offset), :].astype(f32)
            moved = [pltpu.roll(now, i, 1) for i in (1, 2)]
            total = taps[0] * now
            for i in (1, 2):
                total = total + taps[i] * jnp.where(lane < i, before[i - 1], moved[i - 1])
            before = moved
            yield total

    def forward(slot, offset, load):
        for a in range(8):
            values = []
            for q in range(4):
                value = load(a + 8 * q)
                angle = -2.0 * math.pi * q / 16
                values.append((value * math.cos(angle), value * math.sin(angle)) if q else (value, jnp.zeros_like(value)))
            for m, value in enumerate(small_transform(values, -1)):
                real, imag = turned(value, -a * (4 * m + 1) / 128)
                first_ref[m, a, 0] = real
                first_ref[m, a, 1] = imag
        for m in range(4):
            values = [(first_ref[m, a, 0], first_ref[m, a, 1]) for a in range(8)]
            for p, (real, imag) in enumerate(small_transform(values, -1)):
                j = 4 * p + m
                c, s = twists_ref[j, 0][None, :], twists_ref[j, 1][None, :]
                for half, part in enumerate((real * c + imag * s, imag * c - real * s)):
                    high, low = split(part)
                    left_ref[slot, 0, rows_of(j, offset), half * ROWS : (half + 1) * ROWS] = high
                    left_ref[slot, 1, rows_of(j, offset), half * ROWS : (half + 1) * ROWS] = low

    @pl.loop(0, GROUP // SLAB)
    def _(step):
        offset = pl.multiple_of(step * SLAB, SLAB)
        for s, (key, value) in enumerate(zip(short(0, offset), short(1, offset))):
            gated_ref[s, pl.ds(offset, SLAB), :] = key * value
        forward(0, offset, lambda s: gated_ref[s, pl.ds(offset, SLAB), :])
        forward(1, offset, lambda s: x_ref[s, rows_of(SENT - 1, offset), :].astype(f32))

    matrix = jnp.concatenate([high_ref[...], low_ref[...], high_ref[...]], axis=0)

    def product(high, low):
        return jnp.dot(jnp.concatenate([low, high, high], axis=1), matrix, preferred_element_type=f32)

    block = 256
    blocks = [pl.ds(start, block) for start in range(0, PARTS * GROUP, block)]
    for rows in blocks:
        signal = product(left_ref[0, 0, rows, :], left_ref[0, 1, rows, :])
        taps = product(left_ref[1, 0, rows, :], left_ref[1, 1, rows, :])
        a, b = signal[:, :ROWS], signal[:, ROWS:]
        c, d = taps[:, :ROWS], taps[:, ROWS:]
        real, imag = split((a * c - b * d) * (1.0 / POINTS)), split((a * d + b * c) * (-1.0 / POINTS))
        left_ref[0, 0, rows, :] = jnp.concatenate([real[0], imag[0]], axis=1)
        left_ref[0, 1, rows, :] = jnp.concatenate([real[1], imag[1]], axis=1)
    for rows in blocks:
        back_ref[rows, :] = product(left_ref[0, 0, rows, :], left_ref[0, 1, rows, :])

    @pl.loop(0, GROUP // SLAB)
    def _(step):
        offset = pl.multiple_of(step * SLAB, SLAB)
        for m in range(4):
            values = []
            for p in range(8):
                j = 4 * p + m
                real = back_ref[rows_of(j, offset), :ROWS]
                imag = -back_ref[rows_of(j, offset), ROWS:]
                c, s = twists_ref[j, 0][None, :], twists_ref[j, 1][None, :]
                values.append((real * c - imag * s, real * s + imag * c))
            for a, value in enumerate(small_transform(values, 1)):
                real, imag = turned(value, a * (4 * m + 1) / 128)
                first_ref[m, a, 0] = real
                first_ref[m, a, 1] = imag
        skip = skip_ref[pl.ds(offset, SLAB), :]
        for a in range(8):
            values = [(first_ref[m, a, 0], first_ref[m, a, 1]) for m in range(4)]
            for q, (real, imag) in enumerate(small_transform(values, 1)):
                angle = 2.0 * math.pi * q / 16
                conv = real * math.cos(angle) - imag * math.sin(angle) if q else real
                s = a + 8 * q
                gated = gated_ref[s, pl.ds(offset, SLAB), :]
                out_ref[s, pl.ds(offset, SLAB), :] = (conv + skip * gated).astype(bf16)

    for _, _, copy in copies:
        copy.wait()


def fetch(weights_ref, target_ref, sems, away, pieces, first=0):
    columns = (lax.axis_index("ch") + away) % RING * WIDE
    copies = []
    for i, (start, stop) in enumerate(pieces):
        source = weights_ref.at[:, pl.ds(pl.multiple_of(columns + start, 128), stop - start)]
        target = target_ref.at[:, start - first : stop - first]
        copies.append((start, stop, pltpu.make_async_copy(source, target, sems.at[i])))
        copies[-1][2].start()
    return copies


def part_of(rows_ref, held_ref, start, stop):
    return jnp.dot(rows_ref[...], held_ref[:, start:stop], preferred_element_type=f32)


def mixing_kernel(outer_ref, query_ref, held_ref, up_ref, rows_ref):
    rows_ref[...] = (query_ref[...] * outer_ref[...].T.astype(f32)).astype(bf16)
    for start, stop in LEFT:
        up_ref[:, start:stop] = part_of(rows_ref, held_ref, start, stop).astype(bf16)


def far_kernel(rows_ref, rest_ref, down_ref):
    for start, stop in RIGHT:
        down_ref[:, start - UP : stop - UP] = part_of(rows_ref, rest_ref, start - UP, stop - UP).astype(bf16)


def near_kernel(rows_ref, near_ref, up_ref, down_ref):
    for start, stop in RIGHT:
        up_ref[:, start - UP : stop - UP] = part_of(rows_ref, near_ref, start, stop).astype(bf16)
    for start, stop in LEFT:
        down_ref[:, start:stop] = part_of(rows_ref, near_ref, start, stop).astype(bf16)


def adding_kernel(rows_ref, held_ref, arrived_ref, out_ref, *, pieces):
    first = pieces[0][0]
    for start, stop in pieces:
        here = slice(start - first, stop - first)
        total = part_of(rows_ref, held_ref, start, stop)
        out_ref[:, here] = (total + arrived_ref[:, here].astype(f32)).astype(bf16)


def own_kernel(rows_ref, near_up_ref, near_down_ref, weights_ref, out_ref, held_ref, sems):
    for start, stop, copy in fetch(weights_ref, held_ref, sems, 0, LEFT + RIGHT):
        copy.wait()
        arrived = near_down_ref[:, start:stop] if start < UP else near_up_ref[:, start - UP : stop - UP]
        out_ref[:, start:stop] = part_of(rows_ref, held_ref, start, stop) + arrived.astype(f32)


def last_kernel(own_ref, both_up_ref, both_down_ref, out_ref, rows_ref, sems):
    copies = []
    for start in range(0, ROWS, LAST):
        here = slice(start, start + LAST)
        for part, arrived_ref in ((slice(0, UP), both_up_ref), (slice(UP, WIDE), both_down_ref)):
            rows_ref[here, part] = (own_ref[here, part] + arrived_ref[here, :].astype(f32)).astype(bf16)
        copies.append(pltpu.make_async_copy(rows_ref.at[here], out_ref.at[here], sems.at[start // LAST]))
        copies[-1].start()
    for copy in copies:
        copy.wait()


LAST = 32
TABLES = 4
RING = 4
WIDE = 2048
UP = 1152
LEFT = ((0, 640), (640, UP))
RIGHT = ((UP, 1664), (1664, WIDE))
SENT = 3
EDGE = 16
VMEM = pl.BlockSpec(memory_space=pltpu.VMEM)
HBM = pl.BlockSpec(memory_space=pltpu.HBM)


def share(kernel, arrays, outs, held):
    return pl.pallas_call(
        kernel,
        in_specs=[VMEM] * (len(arrays) - 1) + [HBM],
        out_specs=[VMEM] * len(outs),
        out_shape=[pltpu.VMEM(shape, dtype) for shape, dtype in outs],
        scratch_shapes=[
            pltpu.VMEM((arrays[-1].shape[0], held), bf16),
            pltpu.SemaphoreType.DMA((2 * len(LEFT) + len(RIGHT),)),
        ],
        cost_estimate=pl.CostEstimate(flops=2**31, bytes_accessed=2**21, transcendentals=0),
        compiler_params=pltpu.CompilerParams(vmem_limit_bytes=16 * 2**20),
    )(*arrays)


def plain(kernel, arrays, outs):
    return pl.pallas_call(
        kernel,
        in_specs=[VMEM] * len(arrays),
        out_specs=[VMEM] * len(outs),
        out_shape=[pltpu.VMEM(shape, dtype) for shape, dtype in outs],
        cost_estimate=pl.CostEstimate(flops=2**31, bytes_accessed=2**21, transcendentals=0),
        compiler_params=pltpu.CompilerParams(vmem_limit_bytes=8 * 2**20),
    )(*arrays)


def project(outer, query, weights, held, rest, near, later):
    up = [(i, (i + 1) % RING) for i in range(RING)]
    down = [(i, (i - 1) % RING) for i in range(RING)]
    left, right = ((ROWS, UP), bf16), ((ROWS, WIDE - UP), bf16)
    far_up, rows = plain(mixing_kernel, (outer, query, held), [left, (query.shape, bf16)])
    far_up = lax.ppermute(far_up, "ch", up)
    (far_down,) = plain(far_kernel, (rows, rest), [right])
    far_down = lax.ppermute(far_down, "ch", down)
    near_up, near_down = plain(near_kernel, (rows, near), [right, left])
    near_up = lax.ppermute(near_up, "ch", up)
    near_down = lax.ppermute(near_down, "ch", down)
    (both_up,) = plain(functools.partial(adding_kernel, pieces=LEFT), (rows, later, far_up), [left])
    both_up = lax.ppermute(both_up, "ch", up)
    (both_down,) = plain(functools.partial(adding_kernel, pieces=RIGHT), (rows, later, far_down), [right])
    both_down = lax.ppermute(both_down, "ch", down)
    (own,) = share(own_kernel, (rows, near_up, near_down, weights), [((ROWS, WIDE), f32)], WIDE)
    return pl.pallas_call(
        last_kernel,
        in_specs=[VMEM] * 3,
        out_specs=HBM,
        out_shape=jax.ShapeDtypeStruct((ROWS, WIDE), bf16),
        scratch_shapes=[pltpu.VMEM((ROWS, WIDE), bf16), pltpu.SemaphoreType.DMA((ROWS // LAST,))],
        compiler_params=pltpu.CompilerParams(vmem_limit_bytes=16 * 2**20),
    )(own, both_up, both_down)


def stage(after, weights, *arrays):
    arrays = [pltpu.with_memory_space_constraint(array, pltpu.HBM) for array in arrays]
    parts = [pltpu.HBM((weights.shape[0], wide), bf16) for wide in (WIDE - UP, WIDE, WIDE)]
    return pl.pallas_call(
        stage_kernel,
        in_specs=[pl.BlockSpec(memory_space=pl.ANY)] + [HBM] * (len(arrays) + 1),
        out_specs=[VMEM] * len(arrays) + [HBM] * len(parts),
        out_shape=[pltpu.VMEM(array.shape, array.dtype) for array in arrays] + parts,
        scratch_shapes=[
            pltpu.VMEM((weights.shape[0], 3 * WIDE - UP), bf16),
            pltpu.SemaphoreType.DMA((len(arrays) + 2 * len(LEFT) + 3 * len(RIGHT),)),
        ],
        compiler_params=pltpu.CompilerParams(vmem_limit_bytes=16 * 2**20),
    )(after, *arrays, weights)


def convolve(*arrays):
    channels = arrays[-1].shape[0]
    return pl.pallas_call(
        conv_kernel,
        in_specs=[VMEM] * 6 + [HBM],
        out_specs=[VMEM, VMEM],
        out_shape=[
            pltpu.VMEM((PARTS, GROUP, ROWS), bf16),
            pltpu.VMEM((channels, UP), bf16),
        ],
        scratch_shapes=[
            pltpu.VMEM((PARTS, GROUP, ROWS), f32),
            pltpu.VMEM((4, 8, 2, SLAB, ROWS), f32),
            pltpu.VMEM((2, 2, PARTS * GROUP, 2 * ROWS), bf16),
            pltpu.VMEM((PARTS * GROUP, 2 * ROWS), f32),
            pltpu.SemaphoreType.DMA((len(LEFT),)),
        ],
        compiler_params=pltpu.CompilerParams(vmem_limit_bytes=16 * 2**20),
    )(*arrays)


def on_device(streams, short_taps, long_filter, skip_gain, out_weights):
    channels = streams.shape[2]
    streams = pltpu.with_memory_space_constraint(streams, pltpu.HBM)
    weights = pltpu.with_memory_space_constraint(out_weights, pltpu.HBM)
    packed, edge = pl.pallas_call(
        exchange_kernel,
        in_specs=[HBM, HBM],
        out_specs=[HBM, VMEM],
        out_shape=[
            pltpu.HBM((PARTS, SENT * GROUP, ROWS), bf16),
            pltpu.VMEM((EDGE, channels), bf16),
        ],
        scratch_shapes=[
            pltpu.VMEM((SENT - 1, ROWS, channels), bf16),
            pltpu.VMEM((ROWS, channels), f32),
            pltpu.VMEM((PARTS, SENT * GROUP, ROWS), bf16),
            pltpu.SemaphoreType.DMA((SENT + 1,)),
            pltpu.SemaphoreType.DMA((SENT,)),
        ],
        compiler_params=pltpu.CompilerParams(vmem_limit_bytes=8 * 2**20),
    )(streams, pltpu.with_memory_space_constraint(long_filter, pltpu.HBM))
    high, low, twists = (jnp.asarray(table) for table in tables())
    high, low, twists, short_taps, *parts = stage(edge, weights, high, low, twists, short_taps)
    arrived = lax.all_to_all(packed, "seq", 0, 0, tiled=True)
    edge = lax.ppermute(edge, "seq", [(i, i + 1) for i in range(PARTS - 1)])
    first = lax.axis_index("seq") * GROUP
    taps = lax.dynamic_slice_in_dim(short_taps[1:].reshape((SENT - 1) * SHORT, channels), first, GROUP, 1)
    taps = jnp.broadcast_to(taps[:, :, None], ((SENT - 1) * SHORT, GROUP, ROWS))
    skip = jnp.broadcast_to(lax.dynamic_slice_in_dim(skip_gain, first, GROUP, 0)[:, None], (GROUP, ROWS))
    outer, held = convolve(arrived, taps, skip, high, low, twists, weights)
    query = pl.pallas_call(
        query_kernel,
        in_specs=[HBM, VMEM, VMEM, VMEM],
        out_specs=VMEM,
        out_shape=pltpu.VMEM((ROWS, channels), f32),
        scratch_shapes=[pltpu.VMEM((ROWS, channels), bf16), pltpu.SemaphoreType.DMA((1,))],
        compiler_params=pltpu.CompilerParams(vmem_limit_bytes=8 * 2**20),
    )(streams, edge, short_taps, held)
    outer = lax.all_to_all(outer, "seq", 0, 0, tiled=True)
    return project(outer.reshape(channels, ROWS), query, weights, held, *parts)


def solution(mesh):
    return jax.shard_map(
        on_device,
        mesh=mesh,
        in_specs=(
            P(None, "seq", "ch"),
            P(None, None, "ch"),
            P("seq", "ch"),
            P("ch"),
            P("ch", None),
        ),
        out_specs=P("seq", "ch"),
        check_vma=False,
    )
```

```python
import functools
import math

import jax
import jax.numpy as jnp
import numpy as np
from jax import lax
from jax.experimental import pallas as pl
from jax.experimental.pallas import tpu as pltpu
from jax.sharding import PartitionSpec as P

SHORT = 3
ROWS = 128
PARTS = 32
GROUP = 32
SLAB = 16
POINTS = PARTS * ROWS
f32 = jnp.float32
bf16 = jnp.bfloat16


def tables():
    r = np.arange(ROWS)
    angle = 2.0 * np.pi * (np.outer(r, r) % ROWS) / ROWS
    cosine, sine = np.cos(angle), np.sin(angle)
    matrix = np.block([[cosine, -sine], [sine, cosine]])
    high = matrix.astype(np.float32).astype(bf16)
    low = (matrix - high.astype(np.float64)).astype(np.float32).astype(bf16)
    j = np.arange(PARTS)
    twist = 2.0 * np.pi * np.outer(4 * j + 1, r) / (4 * POINTS)
    twists = np.stack([np.cos(twist), np.sin(twist)], axis=1).astype(np.float32)
    return high, low, twists


def turned(value, turns):
    real, imag = value
    eighth = turns * 8 % 8
    if eighth == 0:
        return real, imag
    if eighth == 2:
        return -imag, real
    if eighth == 4:
        return -real, -imag
    if eighth == 6:
        return imag, -real
    if eighth in (1, 3, 5, 7):
        half = math.sqrt(0.5)
        total, apart = (real + imag) * half, (real - imag) * half
        return {1: (apart, total), 3: (-total, apart), 5: (-apart, -total), 7: (total, -apart)}[int(eighth)]
    c, s = math.cos(2.0 * math.pi * turns), math.sin(2.0 * math.pi * turns)
    return real * c - imag * s, real * s + imag * c


def plus(a, b):
    return a[0] + b[0], a[1] + b[1]


def minus(a, b):
    return a[0] - b[0], a[1] - b[1]


def small_transform(values, sign):
    count = len(values)
    if count == 1:
        return values
    even = small_transform(values[0::2], sign)
    odd = small_transform(values[1::2], sign)
    odd = [turned(value, sign * k / count) for k, value in enumerate(odd)]
    return [plus(a, b) for a, b in zip(even, odd)] + [minus(a, b) for a, b in zip(even, odd)]


def exchange_kernel(streams_ref, filter_ref, out_ref, edge_ref, rows_ref, taps_ref, packed_ref, sems, out_sems):
    copies = [pltpu.make_async_copy(streams_ref.at[i + 1], rows_ref.at[i], sems.at[i]) for i in range(SENT - 1)]
    copies.append(pltpu.make_async_copy(filter_ref, taps_ref, sems.at[SENT - 1]))
    edge = pltpu.make_async_copy(streams_ref.at[0, ROWS - EDGE :], edge_ref, sems.at[SENT])
    for copy in copies:
        copy.start()
    edge.start()
    wide = 8 * GROUP
    leaving = []
    for j, copy in enumerate(copies):
        copy.wait()
        for first in range(0, PARTS * GROUP, wide):
            here = slice(first, first + wide)
            block = rows_ref[j, :, here] if j < SENT - 1 else taps_ref[:, here].astype(bf16)
            parts = pl.ds(first // GROUP, wide // GROUP)
            packed_ref[parts, j * GROUP : (j + 1) * GROUP, :] = block.T.reshape(wide // GROUP, GROUP, ROWS)
        own = (slice(None), slice(j * GROUP, (j + 1) * GROUP))
        leaving.append(pltpu.make_async_copy(packed_ref.at[own], out_ref.at[own], out_sems.at[j]))
        leaving[-1].start()
    edge.wait()
    for copy in leaving:
        copy.wait()


def stage_kernel(*refs):
    sems, bounce_ref = refs[-1], refs[-2]
    tables_in, weights_ref = refs[1 : 1 + TABLES], refs[1 + TABLES]
    tables_out = refs[2 + TABLES : 2 + 2 * TABLES]
    rest_ref, near_ref = refs[-4:-2]
    copies = [
        pltpu.make_async_copy(source, target, sems.at[i]) for i, (source, target) in enumerate(zip(tables_in, tables_out))
    ]
    for copy in copies:
        copy.start()
    count, arriving = TABLES, []
    for target_ref, at, away, pieces, first in (
        (near_ref, 0, 1, RIGHT, 0), (near_ref, 0, RING - 1, LEFT, 0), (rest_ref, WIDE, 2, RIGHT, UP),
    ):
        held_ref = bounce_ref.at[:, at : at + target_ref.shape[1]]
        for start, stop, copy in fetch(weights_ref, held_ref, sems.at[count:], away, pieces, first):
            here = slice(start - first, stop - first)
            arriving.append((copy, pltpu.make_async_copy(held_ref.at[:, here], target_ref.at[:, here], sems.at[count])))
            count += 1
    for copy, onward in arriving:
        copy.wait()
        onward.start()
        copies.append(onward)
    for copy in copies:
        copy.wait()


def later_kernel(held_ref, weights_ref, later_ref, bounce_ref, sems):
    arriving = fetch(weights_ref, bounce_ref, sems, 1, LEFT)
    arriving += fetch(weights_ref, bounce_ref, sems.at[len(LEFT) :], RING - 1, RIGHT)
    leaving = []
    for i, (start, stop, copy) in enumerate(arriving):
        copy.wait()
        here = slice(start, stop)
        leaving.append(pltpu.make_async_copy(bounce_ref.at[:, here], later_ref.at[:, here], sems.at[i]))
        leaving[-1].start()
    for copy in leaving:
        copy.wait()


def query_kernel(streams_ref, edge_ref, taps_ref, held_ref, out_ref, rows_ref, sem):
    copy = pltpu.make_async_copy(streams_ref.at[0], rows_ref, sem.at[0])
    copy.start()
    copy.wait()
    now = rows_ref[...].astype(f32)
    earlier = edge_ref[...].astype(f32)
    row = lax.broadcasted_iota(jnp.int32, now.shape, 0)
    last, before_last = earlier[EDGE - 1 :, :], earlier[EDGE - 2 : EDGE - 1, :]
    one = jnp.where(row == 0, last, pltpu.roll(now, 1, 0))
    two = jnp.where(row == 0, before_last, jnp.where(row == 1, last, pltpu.roll(now, 2, 0)))
    out_ref[...] = taps_ref[0, 0:1, :] * now + taps_ref[0, 1:2, :] * one + taps_ref[0, 2:3, :] * two


def split(value):
    high = value.astype(bf16)
    return high, (value - high.astype(f32)).astype(bf16)


def conv_kernel(
    x_ref, taps_ref, skip_ref, high_ref, low_ref, twists_ref, edge_ref, weights_ref,
    out_ref, held_ref, gated_ref, first_ref, left_ref, back_ref, sems,
):
    copies = fetch(weights_ref, held_ref, sems, 2, LEFT)
    lane = lax.broadcasted_iota(jnp.int32, (SLAB, ROWS), 1)

    def rows_of(j, offset):
        return pl.ds(pl.multiple_of(j * GROUP + offset, SLAB), SLAB)

    def short(stream, offset):
        taps = [taps_ref[stream * SHORT + i, pl.ds(offset, SLAB), :] for i in range(SHORT)]
        before = [jnp.zeros((SLAB, ROWS), f32)] * 2
        for s in range(PARTS):
            now = x_ref[s, rows_of(stream, offset), :].astype(f32)
            moved = [pltpu.roll(now, i, 1) for i in (1, 2)]
            total = taps[0] * now
            for i in (1, 2):
                total = total + taps[i] * jnp.where(lane < i, before[i - 1], moved[i - 1])
            before = moved
            yield total

    def forward(slot, offset, load):
        for a in range(8):
            values = []
            for q in range(4):
                value = load(a + 8 * q)
                angle = -2.0 * math.pi * q / 16
                values.append((value * math.cos(angle), value * math.sin(angle)) if q else (value, jnp.zeros_like(value)))
            for m, value in enumerate(small_transform(values, -1)):
                real, imag = turned(value, -a * (4 * m + 1) / 128)
                first_ref[m, a, 0] = real
                first_ref[m, a, 1] = imag
        for m in range(4):
            values = [(first_ref[m, a, 0], first_ref[m, a, 1]) for a in range(8)]
            for p, (real, imag) in enumerate(small_transform(values, -1)):
                j = 4 * p + m
                c, s = twists_ref[j, 0][None, :], twists_ref[j, 1][None, :]
                for half, part in enumerate((real * c + imag * s, imag * c - real * s)):
                    high, low = split(part)
                    left_ref[slot, 0, rows_of(j, offset), half * ROWS : (half + 1) * ROWS] = high
                    left_ref[slot, 1, rows_of(j, offset), half * ROWS : (half + 1) * ROWS] = low

    @pl.loop(0, GROUP // SLAB)
    def _(step):
        offset = pl.multiple_of(step * SLAB, SLAB)
        for s, (key, value) in enumerate(zip(short(0, offset), short(1, offset))):
            gated_ref[s, pl.ds(offset, SLAB), :] = key * value
        forward(0, offset, lambda s: gated_ref[s, pl.ds(offset, SLAB), :])
        forward(1, offset, lambda s: x_ref[s, rows_of(SENT - 1, offset), :].astype(f32))

    matrix = jnp.concatenate([high_ref[...], low_ref[...], high_ref[...]], axis=0)

    def product(high, low):
        return jnp.dot(jnp.concatenate([low, high, high], axis=1), matrix, preferred_element_type=f32)

    block = 256
    blocks = [pl.ds(start, block) for start in range(0, PARTS * GROUP, block)]
    for rows in blocks:
        signal = product(left_ref[0, 0, rows, :], left_ref[0, 1, rows, :])
        taps = product(left_ref[1, 0, rows, :], left_ref[1, 1, rows, :])
        a, b = signal[:, :ROWS], signal[:, ROWS:]
        c, d = taps[:, :ROWS], taps[:, ROWS:]
        real, imag = split((a * c - b * d) * (1.0 / POINTS)), split((a * d + b * c) * (-1.0 / POINTS))
        left_ref[0, 0, rows, :] = jnp.concatenate([real[0], imag[0]], axis=1)
        left_ref[0, 1, rows, :] = jnp.concatenate([real[1], imag[1]], axis=1)
    for rows in blocks:
        back_ref[rows, :] = product(left_ref[0, 0, rows, :], left_ref[0, 1, rows, :])

    @pl.loop(0, GROUP // SLAB)
    def _(step):
        offset = pl.multiple_of(step * SLAB, SLAB)
        for m in range(4):
            values = []
            for p in range(8):
                j = 4 * p + m
                real = back_ref[rows_of(j, offset), :ROWS]
                imag = -back_ref[rows_of(j, offset), ROWS:]
                c, s = twists_ref[j, 0][None, :], twists_ref[j, 1][None, :]
                values.append((real * c - imag * s, real * s + imag * c))
            for a, value in enumerate(small_transform(values, 1)):
                real, imag = turned(value, a * (4 * m + 1) / 128)
                first_ref[m, a, 0] = real
                first_ref[m, a, 1] = imag
        skip = skip_ref[pl.ds(offset, SLAB), :]
        for a in range(8):
            values = [(first_ref[m, a, 0], first_ref[m, a, 1]) for m in range(4)]
            for q, (real, imag) in enumerate(small_transform(values, 1)):
                angle = 2.0 * math.pi * q / 16
                conv = real * math.cos(angle) - imag * math.sin(angle) if q else real
                s = a + 8 * q
                gated = gated_ref[s, pl.ds(offset, SLAB), :]
                out_ref[s, pl.ds(offset, SLAB), :] = (conv + skip * gated).astype(bf16)

    for _, _, copy in copies:
        copy.wait()


def fetch(weights_ref, target_ref, sems, away, pieces, first=0):
    columns = (lax.axis_index("ch") + away) % RING * WIDE
    copies = []
    for i, (start, stop) in enumerate(pieces):
        source = weights_ref.at[:, pl.ds(pl.multiple_of(columns + start, 128), stop - start)]
        target = target_ref.at[:, start - first : stop - first]
        copies.append((start, stop, pltpu.make_async_copy(source, target, sems.at[i])))
        copies[-1][2].start()
    return copies


def part_of(rows_ref, held_ref, start, stop):
    return jnp.dot(rows_ref[...], held_ref[:, start:stop], preferred_element_type=f32)


def mixing_kernel(outer_ref, query_ref, held_ref, later_ref, up_ref, rows_ref):
    rows_ref[...] = (query_ref[...] * outer_ref[...].T.astype(f32)).astype(bf16)
    for start, stop in LEFT:
        up_ref[:, start:stop] = part_of(rows_ref, held_ref, start, stop).astype(bf16)


def far_kernel(rows_ref, rest_ref, down_ref):
    for start, stop in RIGHT:
        down_ref[:, start - UP : stop - UP] = part_of(rows_ref, rest_ref, start - UP, stop - UP).astype(bf16)


def near_kernel(rows_ref, near_ref, up_ref, down_ref):
    for start, stop in RIGHT:
        up_ref[:, start - UP : stop - UP] = part_of(rows_ref, near_ref, start, stop).astype(bf16)
    for start, stop in LEFT:
        down_ref[:, start:stop] = part_of(rows_ref, near_ref, start, stop).astype(bf16)


def adding_kernel(rows_ref, later_ref, far_up_ref, far_down_ref, up_ref, down_ref):
    for start, stop in LEFT:
        total = part_of(rows_ref, later_ref, start, stop)
        up_ref[:, start:stop] = (total + far_up_ref[:, start:stop].astype(f32)).astype(bf16)
    for start, stop in RIGHT:
        here = slice(start - UP, stop - UP)
        total = part_of(rows_ref, later_ref, start, stop)
        down_ref[:, here] = (total + far_down_ref[:, here].astype(f32)).astype(bf16)


def own_kernel(rows_ref, near_up_ref, near_down_ref, weights_ref, out_ref, held_ref, sems):
    for start, stop, copy in fetch(weights_ref, held_ref, sems, 0, LEFT + RIGHT):
        copy.wait()
        arrived = near_down_ref[:, start:stop] if start < UP else near_up_ref[:, start - UP : stop - UP]
        out_ref[:, start:stop] = part_of(rows_ref, held_ref, start, stop) + arrived.astype(f32)


def last_kernel(own_ref, both_up_ref, both_down_ref, out_ref, rows_ref, sems):
    copies = []
    for start in range(0, ROWS, LAST):
        here = slice(start, start + LAST)
        for part, arrived_ref in ((slice(0, UP), both_up_ref), (slice(UP, WIDE), both_down_ref)):
            rows_ref[here, part] = (own_ref[here, part] + arrived_ref[here, :].astype(f32)).astype(bf16)
        copies.append(pltpu.make_async_copy(rows_ref.at[here], out_ref.at[here], sems.at[start // LAST]))
        copies[-1].start()
    for copy in copies:
        copy.wait()


LAST = 32
TABLES = 4
RING = 4
WIDE = 2048
UP = 1152
LEFT = ((0, 640), (640, UP))
RIGHT = ((UP, 1664), (1664, WIDE))
SENT = 3
EDGE = 16
VMEM = pl.BlockSpec(memory_space=pltpu.VMEM)
HBM = pl.BlockSpec(memory_space=pltpu.HBM)


def share(kernel, arrays, outs, held):
    return pl.pallas_call(
        kernel,
        in_specs=[VMEM] * (len(arrays) - 1) + [HBM],
        out_specs=[VMEM] * len(outs),
        out_shape=[pltpu.VMEM(shape, dtype) for shape, dtype in outs],
        scratch_shapes=[
            pltpu.VMEM((arrays[-1].shape[0], held), bf16),
            pltpu.SemaphoreType.DMA((2 * len(LEFT) + len(RIGHT),)),
        ],
        cost_estimate=pl.CostEstimate(flops=2**31, bytes_accessed=2**21, transcendentals=0),
        compiler_params=pltpu.CompilerParams(vmem_limit_bytes=16 * 2**20),
    )(*arrays)


def plain(kernel, arrays, outs, last=VMEM):
    return pl.pallas_call(
        kernel,
        in_specs=[VMEM] * (len(arrays) - 1) + [last],
        out_specs=[VMEM] * len(outs),
        out_shape=[pltpu.VMEM(shape, dtype) for shape, dtype in outs],
        cost_estimate=pl.CostEstimate(flops=2**31, bytes_accessed=2**21, transcendentals=0),
        compiler_params=pltpu.CompilerParams(vmem_limit_bytes=8 * 2**20),
    )(*arrays)


def project(outer, query, weights, held, rest, near, later):
    up = [(i, (i + 1) % RING) for i in range(RING)]
    down = [(i, (i - 1) % RING) for i in range(RING)]
    left, right = ((ROWS, UP), bf16), ((ROWS, WIDE - UP), bf16)
    far_up, rows = plain(mixing_kernel, (outer, query, held, pltpu.with_memory_space_constraint(later, pltpu.HBM)), [left, (query.shape, bf16)], HBM)
    far_up = lax.ppermute(far_up, "ch", up)
    (far_down,) = plain(far_kernel, (rows, rest), [right])
    far_down = lax.ppermute(far_down, "ch", down)
    near_up, near_down = plain(near_kernel, (rows, near), [right, left])
    near_up = lax.ppermute(near_up, "ch", up)
    near_down = lax.ppermute(near_down, "ch", down)
    both_up, both_down = plain(adding_kernel, (rows, later, far_up, far_down), [left, right])
    both_up = lax.ppermute(both_up, "ch", up)
    both_down = lax.ppermute(both_down, "ch", down)
    (own,) = share(own_kernel, (rows, near_up, near_down, weights), [((ROWS, WIDE), f32)], WIDE)
    return pl.pallas_call(
        last_kernel,
        in_specs=[VMEM] * 3,
        out_specs=HBM,
        out_shape=jax.ShapeDtypeStruct((ROWS, WIDE), bf16),
        scratch_shapes=[pltpu.VMEM((ROWS, WIDE), bf16), pltpu.SemaphoreType.DMA((ROWS // LAST,))],
        compiler_params=pltpu.CompilerParams(vmem_limit_bytes=16 * 2**20),
    )(own, both_up, both_down)


def stage(after, weights, *arrays):
    arrays = [pltpu.with_memory_space_constraint(array, pltpu.HBM) for array in arrays]
    parts = [pltpu.HBM((weights.shape[0], wide), bf16) for wide in (WIDE - UP, WIDE)]
    return pl.pallas_call(
        stage_kernel,
        in_specs=[pl.BlockSpec(memory_space=pl.ANY)] + [HBM] * (len(arrays) + 1),
        out_specs=[VMEM] * len(arrays) + [HBM] * len(parts),
        out_shape=[pltpu.VMEM(array.shape, array.dtype) for array in arrays] + parts,
        scratch_shapes=[
            pltpu.VMEM((weights.shape[0], 2 * WIDE - UP), bf16),
            pltpu.SemaphoreType.DMA((len(arrays) + len(LEFT) + 2 * len(RIGHT),)),
        ],
        compiler_params=pltpu.CompilerParams(vmem_limit_bytes=16 * 2**20),
    )(after, *arrays, weights)


def convolve(*arrays):
    channels = arrays[-1].shape[0]
    return pl.pallas_call(
        conv_kernel,
        in_specs=[VMEM] * 7 + [HBM],
        out_specs=[VMEM, VMEM],
        out_shape=[
            pltpu.VMEM((PARTS, GROUP, ROWS), bf16),
            pltpu.VMEM((channels, UP), bf16),
        ],
        scratch_shapes=[
            pltpu.VMEM((PARTS, GROUP, ROWS), f32),
            pltpu.VMEM((4, 8, 2, SLAB, ROWS), f32),
            pltpu.VMEM((2, 2, PARTS * GROUP, 2 * ROWS), bf16),
            pltpu.VMEM((PARTS * GROUP, 2 * ROWS), f32),
            pltpu.SemaphoreType.DMA((len(LEFT),)),
        ],
        compiler_params=pltpu.CompilerParams(vmem_limit_bytes=16 * 2**20),
    )(*arrays)


def on_device(streams, short_taps, long_filter, skip_gain, out_weights):
    channels = streams.shape[2]
    streams = pltpu.with_memory_space_constraint(streams, pltpu.HBM)
    weights = pltpu.with_memory_space_constraint(out_weights, pltpu.HBM)
    packed, edge = pl.pallas_call(
        exchange_kernel,
        in_specs=[HBM, HBM],
        out_specs=[HBM, VMEM],
        out_shape=[
            pltpu.HBM((PARTS, SENT * GROUP, ROWS), bf16),
            pltpu.VMEM((EDGE, channels), bf16),
        ],
        scratch_shapes=[
            pltpu.VMEM((SENT - 1, ROWS, channels), bf16),
            pltpu.VMEM((ROWS, channels), f32),
            pltpu.VMEM((PARTS, SENT * GROUP, ROWS), bf16),
            pltpu.SemaphoreType.DMA((SENT + 1,)),
            pltpu.SemaphoreType.DMA((SENT,)),
        ],
        compiler_params=pltpu.CompilerParams(vmem_limit_bytes=8 * 2**20),
    )(streams, pltpu.with_memory_space_constraint(long_filter, pltpu.HBM))
    high, low, twists = (jnp.asarray(table) for table in tables())
    high, low, twists, short_taps, *parts = stage(edge, weights, high, low, twists, short_taps)
    arrived = lax.all_to_all(packed, "seq", 0, 0, tiled=True)
    edge = lax.ppermute(edge, "seq", [(i, i + 1) for i in range(PARTS - 1)])
    first = lax.axis_index("seq") * GROUP
    taps = lax.dynamic_slice_in_dim(short_taps[1:].reshape((SENT - 1) * SHORT, channels), first, GROUP, 1)
    taps = jnp.broadcast_to(taps[:, :, None], ((SENT - 1) * SHORT, GROUP, ROWS))
    skip = jnp.broadcast_to(lax.dynamic_slice_in_dim(skip_gain, first, GROUP, 0)[:, None], (GROUP, ROWS))
    outer, held = convolve(arrived, taps, skip, high, low, twists, edge, weights)
    later = pl.pallas_call(
        later_kernel,
        in_specs=[VMEM, HBM],
        out_specs=HBM,
        out_shape=pltpu.HBM((channels, WIDE), bf16),
        scratch_shapes=[
            pltpu.VMEM((channels, WIDE), bf16),
            pltpu.SemaphoreType.DMA((len(LEFT + RIGHT),)),
        ],
        compiler_params=pltpu.CompilerParams(vmem_limit_bytes=8 * 2**20),
    )(held, weights)
    query = pl.pallas_call(
        query_kernel,
        in_specs=[HBM, VMEM, VMEM, VMEM],
        out_specs=VMEM,
        out_shape=pltpu.VMEM((ROWS, channels), f32),
        scratch_shapes=[pltpu.VMEM((ROWS, channels), bf16), pltpu.SemaphoreType.DMA((1,))],
        compiler_params=pltpu.CompilerParams(vmem_limit_bytes=8 * 2**20),
    )(streams, edge, short_taps, held)
    outer = lax.all_to_all(outer, "seq", 0, 0, tiled=True)
    return project(outer.reshape(channels, ROWS), query, weights, held, *parts, later)


def solution(mesh):
    return jax.shard_map(
        on_device,
        mesh=mesh,
        in_specs=(
            P(None, "seq", "ch"),
            P(None, None, "ch"),
            P("seq", "ch"),
            P("ch"),
            P("ch", None),
        ),
        out_specs=P("seq", "ch"),
        check_vma=False,
    )
```

```python
import functools
import math

import jax
import jax.numpy as jnp
import numpy as np
from jax import lax
from jax.experimental import pallas as pl
from jax.experimental.pallas import tpu as pltpu
from jax.sharding import PartitionSpec as P

SHORT = 3
ROWS = 128
PARTS = 32
GROUP = 32
SLAB = 16
POINTS = PARTS * ROWS
f32 = jnp.float32
bf16 = jnp.bfloat16


def tables():
    r = np.arange(ROWS)
    angle = 2.0 * np.pi * (np.outer(r, r) % ROWS) / ROWS
    cosine, sine = np.cos(angle), np.sin(angle)
    matrix = np.block([[cosine, -sine], [sine, cosine]])
    high = matrix.astype(np.float32).astype(bf16)
    low = (matrix - high.astype(np.float64)).astype(np.float32).astype(bf16)
    j = np.arange(PARTS)
    twist = 2.0 * np.pi * np.outer(4 * j + 1, r) / (4 * POINTS)
    twists = np.stack([np.cos(twist), np.sin(twist)], axis=1).astype(np.float32)
    return high, low, twists


def turned(value, turns):
    real, imag = value
    eighth = turns * 8 % 8
    if eighth == 0:
        return real, imag
    if eighth == 2:
        return -imag, real
    if eighth == 4:
        return -real, -imag
    if eighth == 6:
        return imag, -real
    if eighth in (1, 3, 5, 7):
        half = math.sqrt(0.5)
        total, apart = (real + imag) * half, (real - imag) * half
        return {1: (apart, total), 3: (-total, apart), 5: (-apart, -total), 7: (total, -apart)}[int(eighth)]
    c, s = math.cos(2.0 * math.pi * turns), math.sin(2.0 * math.pi * turns)
    return real * c - imag * s, real * s + imag * c


def plus(a, b):
    return a[0] + b[0], a[1] + b[1]


def minus(a, b):
    return a[0] - b[0], a[1] - b[1]


def small_transform(values, sign):
    count = len(values)
    if count == 1:
        return values
    even = small_transform(values[0::2], sign)
    odd = small_transform(values[1::2], sign)
    odd = [turned(value, sign * k / count) for k, value in enumerate(odd)]
    return [plus(a, b) for a, b in zip(even, odd)] + [minus(a, b) for a, b in zip(even, odd)]


def exchange_kernel(streams_ref, filter_ref, out_ref, edge_ref, rows_ref, taps_ref, packed_ref, sems, out_sems):
    copies = [pltpu.make_async_copy(streams_ref.at[i + 1], rows_ref.at[i], sems.at[i]) for i in range(SENT - 1)]
    copies.append(pltpu.make_async_copy(filter_ref, taps_ref, sems.at[SENT - 1]))
    edge = pltpu.make_async_copy(streams_ref.at[0, ROWS - EDGE :], edge_ref, sems.at[SENT])
    for copy in copies:
        copy.start()
    edge.start()
    wide = 8 * GROUP
    leaving = []
    for j, copy in enumerate(copies):
        copy.wait()
        for first in range(0, PARTS * GROUP, wide):
            here = slice(first, first + wide)
            block = rows_ref[j, :, here] if j < SENT - 1 else taps_ref[:, here].astype(bf16)
            parts = pl.ds(first // GROUP, wide // GROUP)
            packed_ref[parts, j * GROUP : (j + 1) * GROUP, :] = block.T.reshape(wide // GROUP, GROUP, ROWS)
        own = (slice(None), slice(j * GROUP, (j + 1) * GROUP))
        leaving.append(pltpu.make_async_copy(packed_ref.at[own], out_ref.at[own], out_sems.at[j]))
        leaving[-1].start()
    edge.wait()
    for copy in leaving:
        copy.wait()


def stage_kernel(*refs):
    sems, bounce_ref = refs[-1], refs[-2]
    tables_in, weights_ref = refs[1 : 1 + TABLES], refs[1 + TABLES]
    tables_out = refs[2 + TABLES : 2 + 2 * TABLES]
    rest_ref, near_ref, later_ref = refs[-5:-2]
    copies = [
        pltpu.make_async_copy(source, target, sems.at[i]) for i, (source, target) in enumerate(zip(tables_in, tables_out))
    ]
    for copy in copies:
        copy.start()
    count, arriving = TABLES, []
    for target_ref, at, away, pieces, first in (
        (near_ref, 0, 1, RIGHT, 0), (near_ref, 0, RING - 1, LEFT, 0), (rest_ref, WIDE, 2, RIGHT, UP),
        (later_ref, 2 * WIDE - UP, 1, LEFT, 0), (later_ref, 2 * WIDE - UP, RING - 1, RIGHT, 0),
    ):
        held_ref = bounce_ref.at[:, at : at + target_ref.shape[1]]
        for start, stop, copy in fetch(weights_ref, held_ref, sems.at[count:], away, pieces, first):
            here = slice(start - first, stop - first)
            arriving.append((copy, pltpu.make_async_copy(held_ref.at[:, here], target_ref.at[:, here], sems.at[count])))
            count += 1
    for copy, onward in arriving:
        copy.wait()
        onward.start()
        copies.append(onward)
    for copy in copies:
        copy.wait()


def query_kernel(streams_ref, edge_ref, taps_ref, held_ref, out_ref, rows_ref, sem):
    copy = pltpu.make_async_copy(streams_ref.at[0], rows_ref, sem.at[0])
    copy.start()
    copy.wait()
    now = rows_ref[...].astype(f32)
    earlier = edge_ref[...].astype(f32)
    row = lax.broadcasted_iota(jnp.int32, now.shape, 0)
    last, before_last = earlier[EDGE - 1 :, :], earlier[EDGE - 2 : EDGE - 1, :]
    one = jnp.where(row == 0, last, pltpu.roll(now, 1, 0))
    two = jnp.where(row == 0, before_last, jnp.where(row == 1, last, pltpu.roll(now, 2, 0)))
    out_ref[...] = taps_ref[0, 0:1, :] * now + taps_ref[0, 1:2, :] * one + taps_ref[0, 2:3, :] * two


def split(value):
    high = value.astype(bf16)
    return high, (value - high.astype(f32)).astype(bf16)


def conv_kernel(
    x_ref, taps_ref, skip_ref, high_ref, low_ref, twists_ref, weights_ref,
    out_ref, held_ref, gated_ref, first_ref, left_ref, back_ref, outer_ref, sems, out_sems,
):
    copies = fetch(weights_ref, held_ref, sems, 2, LEFT)
    lane = lax.broadcasted_iota(jnp.int32, (SLAB, ROWS), 1)

    def rows_of(j, offset):
        return pl.ds(pl.multiple_of(j * GROUP + offset, SLAB), SLAB)

    def short(stream, offset):
        taps = [taps_ref[stream * SHORT + i, pl.ds(offset, SLAB), :] for i in range(SHORT)]
        before = [jnp.zeros((SLAB, ROWS), f32)] * 2
        for s in range(PARTS):
            now = x_ref[s, rows_of(stream, offset), :].astype(f32)
            moved = [pltpu.roll(now, i, 1) for i in (1, 2)]
            total = taps[0] * now
            for i in (1, 2):
                total = total + taps[i] * jnp.where(lane < i, before[i - 1], moved[i - 1])
            before = moved
            yield total

    def forward(slot, offset, load):
        for a in range(8):
            values = []
            for q in range(4):
                value = load(a + 8 * q)
                angle = -2.0 * math.pi * q / 16
                values.append((value * math.cos(angle), value * math.sin(angle)) if q else (value, jnp.zeros_like(value)))
            for m, value in enumerate(small_transform(values, -1)):
                real, imag = turned(value, -a * (4 * m + 1) / 128)
                first_ref[m, a, 0] = real
                first_ref[m, a, 1] = imag
        for m in range(4):
            values = [(first_ref[m, a, 0], first_ref[m, a, 1]) for a in range(8)]
            for p, (real, imag) in enumerate(small_transform(values, -1)):
                j = 4 * p + m
                c, s = twists_ref[j, 0][None, :], twists_ref[j, 1][None, :]
                for half, part in enumerate((real * c + imag * s, imag * c - real * s)):
                    high, low = split(part)
                    left_ref[slot, 0, rows_of(j, offset), half * ROWS : (half + 1) * ROWS] = high
                    left_ref[slot, 1, rows_of(j, offset), half * ROWS : (half + 1) * ROWS] = low

    @pl.loop(0, GROUP // SLAB)
    def _(step):
        offset = pl.multiple_of(step * SLAB, SLAB)
        for s, (key, value) in enumerate(zip(short(0, offset), short(1, offset))):
            gated_ref[s, pl.ds(offset, SLAB), :] = key * value
        forward(0, offset, lambda s: gated_ref[s, pl.ds(offset, SLAB), :])
        forward(1, offset, lambda s: x_ref[s, rows_of(SENT - 1, offset), :].astype(f32))

    matrix = jnp.concatenate([high_ref[...], low_ref[...], high_ref[...]], axis=0)

    def product(high, low):
        return jnp.dot(jnp.concatenate([low, high, high], axis=1), matrix, preferred_element_type=f32)

    block = 256
    blocks = [pl.ds(start, block) for start in range(0, PARTS * GROUP, block)]
    for rows in blocks:
        signal = product(left_ref[0, 0, rows, :], left_ref[0, 1, rows, :])
        taps = product(left_ref[1, 0, rows, :], left_ref[1, 1, rows, :])
        a, b = signal[:, :ROWS], signal[:, ROWS:]
        c, d = taps[:, :ROWS], taps[:, ROWS:]
        real, imag = split((a * c - b * d) * (1.0 / POINTS)), split((a * d + b * c) * (-1.0 / POINTS))
        left_ref[0, 0, rows, :] = jnp.concatenate([real[0], imag[0]], axis=1)
        left_ref[0, 1, rows, :] = jnp.concatenate([real[1], imag[1]], axis=1)
    for rows in blocks:
        back_ref[rows, :] = product(left_ref[0, 0, rows, :], left_ref[0, 1, rows, :])

    def leaving(step):
        here = pl.ds(pl.multiple_of(step * SLAB, SLAB), SLAB)
        return pltpu.make_async_copy(outer_ref.at[:, here, :], out_ref.at[:, here, :], out_sems.at[step])

    @pl.loop(0, GROUP // SLAB)
    def _(step):
        offset = pl.multiple_of(step * SLAB, SLAB)
        for m in range(4):
            values = []
            for p in range(8):
                j = 4 * p + m
                real = back_ref[rows_of(j, offset), :ROWS]
                imag = -back_ref[rows_of(j, offset), ROWS:]
                c, s = twists_ref[j, 0][None, :], twists_ref[j, 1][None, :]
                values.append((real * c - imag * s, real * s + imag * c))
            for a, value in enumerate(small_transform(values, 1)):
                real, imag = turned(value, a * (4 * m + 1) / 128)
                first_ref[m, a, 0] = real
                first_ref[m, a, 1] = imag
        skip = skip_ref[pl.ds(offset, SLAB), :]
        for a in range(8):
            values = [(first_ref[m, a, 0], first_ref[m, a, 1]) for m in range(4)]
            for q, (real, imag) in enumerate(small_transform(values, 1)):
                angle = 2.0 * math.pi * q / 16
                conv = real * math.cos(angle) - imag * math.sin(angle) if q else real
                s = a + 8 * q
                gated = gated_ref[s, pl.ds(offset, SLAB), :]
                outer_ref[s, pl.ds(offset, SLAB), :] = (conv + skip * gated).astype(bf16)
        leaving(step).start()

    for step in range(GROUP // SLAB):
        leaving(step).wait()
    for _, _, copy in copies:
        copy.wait()


def fetch(weights_ref, target_ref, sems, away, pieces, first=0):
    columns = (lax.axis_index("ch") + away) % RING * WIDE
    copies = []
    for i, (start, stop) in enumerate(pieces):
        source = weights_ref.at[:, pl.ds(pl.multiple_of(columns + start, 128), stop - start)]
        target = target_ref.at[:, start - first : stop - first]
        copies.append((start, stop, pltpu.make_async_copy(source, target, sems.at[i])))
        copies[-1][2].start()
    return copies


def part_of(rows_ref, held_ref, start, stop):
    return jnp.dot(rows_ref[...], held_ref[:, start:stop], preferred_element_type=f32)


def mixing_kernel(outer_ref, query_ref, held_ref, up_ref, rows_ref):
    rows_ref[...] = (query_ref[...] * outer_ref[...].T.astype(f32)).astype(bf16)
    for start, stop in LEFT:
        up_ref[:, start:stop] = part_of(rows_ref, held_ref, start, stop).astype(bf16)


def far_kernel(rows_ref, rest_ref, down_ref):
    for start, stop in RIGHT:
        down_ref[:, start - UP : stop - UP] = part_of(rows_ref, rest_ref, start - UP, stop - UP).astype(bf16)


def near_kernel(rows_ref, near_ref, up_ref, down_ref):
    for start, stop in RIGHT:
        up_ref[:, start - UP : stop - UP] = part_of(rows_ref, near_ref, start, stop).astype(bf16)
    for start, stop in LEFT:
        down_ref[:, start:stop] = part_of(rows_ref, near_ref, start, stop).astype(bf16)


def adding_kernel(rows_ref, later_ref, far_up_ref, far_down_ref, up_ref, down_ref):
    for start, stop in LEFT:
        total = part_of(rows_ref, later_ref, start, stop)
        up_ref[:, start:stop] = (total + far_up_ref[:, start:stop].astype(f32)).astype(bf16)
    for start, stop in RIGHT:
        here = slice(start - UP, stop - UP)
        total = part_of(rows_ref, later_ref, start, stop)
        down_ref[:, here] = (total + far_down_ref[:, here].astype(f32)).astype(bf16)


def own_kernel(rows_ref, near_up_ref, near_down_ref, weights_ref, out_ref, held_ref, sems):
    for start, stop, copy in fetch(weights_ref, held_ref, sems, 0, LEFT + RIGHT):
        copy.wait()
        arrived = near_down_ref[:, start:stop] if start < UP else near_up_ref[:, start - UP : stop - UP]
        out_ref[:, start:stop] = part_of(rows_ref, held_ref, start, stop) + arrived.astype(f32)


def last_kernel(own_ref, both_up_ref, both_down_ref, out_ref, rows_ref, sems):
    copies = []
    for start in range(0, ROWS, LAST):
        here = slice(start, start + LAST)
        for part, arrived_ref in ((slice(0, UP), both_up_ref), (slice(UP, WIDE), both_down_ref)):
            rows_ref[here, part] = (own_ref[here, part] + arrived_ref[here, :].astype(f32)).astype(bf16)
        copies.append(pltpu.make_async_copy(rows_ref.at[here], out_ref.at[here], sems.at[start // LAST]))
        copies[-1].start()
    for copy in copies:
        copy.wait()


LAST = 32
TABLES = 4
RING = 4
WIDE = 2048
UP = 1152
LEFT = ((0, 640), (640, UP))
RIGHT = ((UP, 1664), (1664, WIDE))
SENT = 3
EDGE = 16
VMEM = pl.BlockSpec(memory_space=pltpu.VMEM)
HBM = pl.BlockSpec(memory_space=pltpu.HBM)


def share(kernel, arrays, outs, held):
    return pl.pallas_call(
        kernel,
        in_specs=[VMEM] * (len(arrays) - 1) + [HBM],
        out_specs=[VMEM] * len(outs),
        out_shape=[pltpu.VMEM(shape, dtype) for shape, dtype in outs],
        scratch_shapes=[
            pltpu.VMEM((arrays[-1].shape[0], held), bf16),
            pltpu.SemaphoreType.DMA((2 * len(LEFT) + len(RIGHT),)),
        ],
        cost_estimate=pl.CostEstimate(flops=2**31, bytes_accessed=2**21, transcendentals=0),
        compiler_params=pltpu.CompilerParams(vmem_limit_bytes=16 * 2**20),
    )(*arrays)


def plain(kernel, arrays, outs):
    return pl.pallas_call(
        kernel,
        in_specs=[VMEM] * len(arrays),
        out_specs=[VMEM] * len(outs),
        out_shape=[pltpu.VMEM(shape, dtype) for shape, dtype in outs],
        cost_estimate=pl.CostEstimate(flops=2**31, bytes_accessed=2**21, transcendentals=0),
        compiler_params=pltpu.CompilerParams(vmem_limit_bytes=8 * 2**20),
    )(*arrays)


def project(outer, query, weights, held, rest, near, later):
    up = [(i, (i + 1) % RING) for i in range(RING)]
    down = [(i, (i - 1) % RING) for i in range(RING)]
    left, right = ((ROWS, UP), bf16), ((ROWS, WIDE - UP), bf16)
    far_up, rows = plain(mixing_kernel, (outer, query, held), [left, (query.shape, bf16)])
    far_up = lax.ppermute(far_up, "ch", up)
    (far_down,) = plain(far_kernel, (rows, rest), [right])
    far_down = lax.ppermute(far_down, "ch", down)
    near_up, near_down = plain(near_kernel, (rows, near), [right, left])
    near_up = lax.ppermute(near_up, "ch", up)
    near_down = lax.ppermute(near_down, "ch", down)
    both_up, both_down = plain(adding_kernel, (rows, later, far_up, far_down), [left, right])
    both_up = lax.ppermute(both_up, "ch", up)
    both_down = lax.ppermute(both_down, "ch", down)
    (own,) = share(own_kernel, (rows, near_up, near_down, weights), [((ROWS, WIDE), f32)], WIDE)
    return pl.pallas_call(
        last_kernel,
        in_specs=[VMEM] * 3,
        out_specs=HBM,
        out_shape=jax.ShapeDtypeStruct((ROWS, WIDE), bf16),
        scratch_shapes=[pltpu.VMEM((ROWS, WIDE), bf16), pltpu.SemaphoreType.DMA((ROWS // LAST,))],
        compiler_params=pltpu.CompilerParams(vmem_limit_bytes=16 * 2**20),
    )(own, both_up, both_down)


def stage(after, weights, *arrays):
    arrays = [pltpu.with_memory_space_constraint(array, pltpu.HBM) for array in arrays]
    parts = [pltpu.HBM((weights.shape[0], wide), bf16) for wide in (WIDE - UP, WIDE, WIDE)]
    return pl.pallas_call(
        stage_kernel,
        in_specs=[pl.BlockSpec(memory_space=pl.ANY)] + [HBM] * (len(arrays) + 1),
        out_specs=[VMEM] * len(arrays) + [HBM] * len(parts),
        out_shape=[pltpu.VMEM(array.shape, array.dtype) for array in arrays] + parts,
        scratch_shapes=[
            pltpu.VMEM((weights.shape[0], 3 * WIDE - UP), bf16),
            pltpu.SemaphoreType.DMA((len(arrays) + 2 * len(LEFT) + 3 * len(RIGHT),)),
        ],
        compiler_params=pltpu.CompilerParams(vmem_limit_bytes=16 * 2**20),
    )(after, *arrays, weights)


def convolve(*arrays):
    channels = arrays[-1].shape[0]
    return pl.pallas_call(
        conv_kernel,
        in_specs=[VMEM] * 6 + [HBM],
        out_specs=[HBM, VMEM],
        out_shape=[
            pltpu.HBM((PARTS, GROUP, ROWS), bf16),
            pltpu.VMEM((channels, UP), bf16),
        ],
        scratch_shapes=[
            pltpu.VMEM((PARTS, GROUP, ROWS), f32),
            pltpu.VMEM((4, 8, 2, SLAB, ROWS), f32),
            pltpu.VMEM((2, 2, PARTS * GROUP, 2 * ROWS), bf16),
            pltpu.VMEM((PARTS * GROUP, 2 * ROWS), f32),
            pltpu.VMEM((PARTS, GROUP, ROWS), bf16),
            pltpu.SemaphoreType.DMA((len(LEFT),)),
            pltpu.SemaphoreType.DMA((GROUP // SLAB,)),
        ],
        compiler_params=pltpu.CompilerParams(vmem_limit_bytes=16 * 2**20),
    )(*arrays)


def on_device(streams, short_taps, long_filter, skip_gain, out_weights):
    channels = streams.shape[2]
    streams = pltpu.with_memory_space_constraint(streams, pltpu.HBM)
    weights = pltpu.with_memory_space_constraint(out_weights, pltpu.HBM)
    packed, edge = pl.pallas_call(
        exchange_kernel,
        in_specs=[HBM, HBM],
        out_specs=[HBM, VMEM],
        out_shape=[
            pltpu.HBM((PARTS, SENT * GROUP, ROWS), bf16),
            pltpu.VMEM((EDGE, channels), bf16),
        ],
        scratch_shapes=[
            pltpu.VMEM((SENT - 1, ROWS, channels), bf16),
            pltpu.VMEM((ROWS, channels), f32),
            pltpu.VMEM((PARTS, SENT * GROUP, ROWS), bf16),
            pltpu.SemaphoreType.DMA((SENT + 1,)),
            pltpu.SemaphoreType.DMA((SENT,)),
        ],
        compiler_params=pltpu.CompilerParams(vmem_limit_bytes=8 * 2**20),
    )(streams, pltpu.with_memory_space_constraint(long_filter, pltpu.HBM))
    high, low, twists = (jnp.asarray(table) for table in tables())
    high, low, twists, short_taps, *parts = stage(edge, weights, high, low, twists, short_taps)
    arrived = lax.all_to_all(packed, "seq", 0, 0, tiled=True)
    edge = lax.ppermute(edge, "seq", [(i, i + 1) for i in range(PARTS - 1)])
    first = lax.axis_index("seq") * GROUP
    taps = lax.dynamic_slice_in_dim(short_taps[1:].reshape((SENT - 1) * SHORT, channels), first, GROUP, 1)
    taps = jnp.broadcast_to(taps[:, :, None], ((SENT - 1) * SHORT, GROUP, ROWS))
    skip = jnp.broadcast_to(lax.dynamic_slice_in_dim(skip_gain, first, GROUP, 0)[:, None], (GROUP, ROWS))
    outer, held = convolve(arrived, taps, skip, high, low, twists, weights)
    query = pl.pallas_call(
        query_kernel,
        in_specs=[HBM, VMEM, VMEM, VMEM],
        out_specs=VMEM,
        out_shape=pltpu.VMEM((ROWS, channels), f32),
        scratch_shapes=[pltpu.VMEM((ROWS, channels), bf16), pltpu.SemaphoreType.DMA((1,))],
        compiler_params=pltpu.CompilerParams(vmem_limit_bytes=8 * 2**20),
    )(streams, edge, short_taps, held)
    outer = lax.all_to_all(outer, "seq", 0, 0, tiled=True)
    return project(outer.reshape(channels, ROWS), query, weights, held, *parts)


def solution(mesh):
    return jax.shard_map(
        on_device,
        mesh=mesh,
        in_specs=(
            P(None, "seq", "ch"),
            P(None, None, "ch"),
            P("seq", "ch"),
            P("ch"),
            P("ch", None),
        ),
        out_specs=P("seq", "ch"),
        check_vma=False,
    )
```
